32 devices in a mesh: section: 4 (over y, x), ctx: 8 (over z, core).
Axes of the slice: x: 2, y: 2, z: 4, core: 2. Of those that a mesh axis runs over, the one named last changes fastest.
Arguments:
- latent_state: bfloat16 [4, 1280, 1536], P('section', 'ctx'), may hold values from -20 to 20
- lead_step: int32 [4], replicated, may hold values from 0 to 3, each once
- tail_qkv: bfloat16 [1536, 1280], P(('section', 'ctx')), may hold values from -0.15625 to 0.15625
- tail_out: bfloat16 [1536, 768], P(('section', 'ctx')), may hold values from -0.21875 to 0.21875
- head_qkv: bfloat16 [1536, 1280], P(('section', 'ctx')), may hold values from -0.15625 to 0.15625
- head_out: bfloat16 [1536, 768], P(('section', 'ctx')), may hold values from -0.21875 to 0.21875
- modulation: float32 [2, 2, 5, 1536], replicated, may hold values from 0.5 to 1.5
- qk_gain: float32 [2, 2, 128], replicated, may hold values from 1 to 2
Outputs:
- tail_state: bfloat16 [4, 1280, 1536], P('section', 'ctx')
- head_state: bfloat16 [4, 1280, 1536], P('section', 'ctx')
The draws below stay inside these ranges and needn't reach their ends.
Inputs may be any that keep to these rules, and one draw needn't show every extreme that they name: `lead_step`: every section holds a different lead time.
All inputs are finite; a program needn't handle non-finite values.
Results may differ from the reference program's by a relative error of at most 0.01.
Values may be sent and summed in bfloat16 or wider, within the bound.
A program may use at most 64 MiB of HBM per device.

```python
import math
import jax
import jax.numpy as jnp
from jax import lax

D = 1536
QH = 6
KVH = 2
HD = 128
QW = 768
KW = 256
SEQ = 1280
LEADS = 5
N_SECTION = 4
N_CTX = 8


def draw_latent_state(key, part):
    subkeys = jax.random.split(key, 3)
    row_scale = jnp.exp(jax.random.uniform(subkeys[0], (N_SECTION, SEQ, 1), jnp.float32, math.log(0.3), math.log(3.0)))
    col_scale = jnp.exp(jax.random.uniform(subkeys[1], (1, 1, D), jnp.float32, math.log(0.3), math.log(3.0)))
    values = jnp.clip(jax.random.normal(subkeys[2], (N_SECTION, SEQ, D), jnp.float32), -3.0, 3.0)
    return (0.5 * row_scale * col_scale * values).astype(jnp.bfloat16)


def block_scale(stream_key, dims, shards, least, high):
    def one(position, blocks):
        heights = jax.random.uniform(jax.random.fold_in(jax.random.fold_in(stream_key, 6), position), (blocks,), jnp.float32, least / len(shards), high / len(shards))
        return jnp.repeat(jnp.exp(heights), dims[position] // blocks).reshape((-1,) + (1,) * (len(dims) - position - 1))

    level = one(*shards[0])
    for cut in shards[1:]:
        level = level * one(*cut)
    return level


def normal_values(stream_key, shape, spread, bound, cuts=(), held_as=jnp.bfloat16):
    level = block_scale(stream_key, shape, cuts, -0.22, 0.18) if cuts else 1.0
    entries = jax.random.normal(stream_key, shape, jnp.float32) * spread * level
    return jnp.minimum(jnp.maximum(entries, -bound), bound).astype(held_as)


def setup_inputs(seed: int = 0) -> dict:
    key_list = jax.random.split(jax.random.key(seed), 9)
    return {
        "latent_state": draw_latent_state(jax.random.fold_in(key_list[8], 71), 0),
        "lead_step": jax.random.permutation(key_list[1], N_SECTION).astype(jnp.int32),
        "tail_qkv": normal_values(key_list[2], (D, QW + 2 * KW), D ** -0.5, 0.15625, ((0, 32),)),
        "tail_out": normal_values(key_list[3], (D, QW), QW ** -0.5, 0.21875, ((0, 32),)),
        "head_qkv": normal_values(key_list[4], (D, QW + 2 * KW), D ** -0.5, 0.15625, ((0, 32),)),
        "head_out": normal_values(key_list[5], (D, QW), QW ** -0.5, 0.21875, ((0, 32),)),
        "modulation": jnp.clip(1.0 + 0.1 * jax.random.normal(key_list[6], (2, 2, LEADS, D), jnp.float32), 0.5, 1.5),
        "qk_gain": jnp.clip(jnp.exp(jax.random.uniform(key_list[7], (2, 2, HD), jnp.float32, math.log(1.0), math.log(2.0))), 1.0, 2.0),
    }


def qk_normal(values, gain_row):
    factor = lax.rsqrt(lax.optimization_barrier(jnp.mean(values * values, axis=-1, keepdims=True)) + 1e-06)
    return (values * factor * gain_row).astype(jnp.bfloat16)

def attention_layer(inputs, w_joined, w_output, norm_gain, res_gate, q_gain, k_gain):
    seq_len = inputs.shape[0]
    groups = QH // KVH
    widened = inputs.astype(jnp.float32)
    factor = lax.rsqrt(lax.optimization_barrier(jnp.mean(widened * widened, axis=-1, keepdims=True)) + 1e-06)
    normed = (widened * factor * norm_gain).astype(jnp.bfloat16)
    projected = jnp.dot(normed, w_joined, preferred_element_type=jnp.float32)
    queries = qk_normal(projected[:, :QH * HD].reshape(seq_len, KVH, groups, HD), q_gain)
    key_rows = qk_normal(projected[:, QH * HD:(QH + KVH) * HD].reshape(seq_len, KVH, HD), k_gain)
    val_rows = projected[:, (QH + KVH) * HD:].astype(jnp.bfloat16).reshape(seq_len, KVH, HD)
    key_wide = lax.optimization_barrier(key_rows).astype(jnp.float32)
    val_wide = lax.optimization_barrier(val_rows).astype(jnp.float32)
    query_blocks = queries.reshape(N_CTX, seq_len // N_CTX, KVH, groups, HD)
    score_scale = float(HD) ** (-0.5)

    def per_block(query_block):
        query_wide = lax.optimization_barrier(query_block).astype(jnp.float32)
        scores = jnp.einsum('tkgd,skd->tkgs', query_wide, key_wide) * score_scale
        weights = jnp.exp(scores)
        denominator = lax.optimization_barrier(jnp.sum(weights, axis=-1))
        rounded = lax.optimization_barrier(weights.astype(jnp.bfloat16)).astype(jnp.float32)
        numerator = jnp.einsum('tkgs,skd->tkgd', rounded, val_wide)
        return (numerator / denominator[..., None]).astype(jnp.bfloat16)
    attended = lax.map(per_block, query_blocks).reshape(seq_len, QH * HD)
    update = jnp.dot(attended, w_output.T, preferred_element_type=jnp.float32)
    return (widened + res_gate * update).astype(jnp.bfloat16)

def reference(latent_state, lead_step, tail_qkv, tail_out, head_qkv, head_out, modulation, qk_gain):
    section_count = latent_state.shape[0]
    tails = []
    for section_pos in range(section_count):
        lead_now = lead_step[section_pos]
        tails.append(attention_layer(latent_state[section_pos], tail_qkv, tail_out, modulation[0, 0, lead_now], modulation[0, 1, lead_now], qk_gain[0, 0], qk_gain[0, 1]))
    heads = []
    for section_pos in range(section_count):
        sender = (section_pos - 1) % section_count
        lead_next = lead_step[sender] + 1
        heads.append(attention_layer(tails[sender], head_qkv, head_out, modulation[1, 0, lead_next], modulation[1, 1, lead_next], qk_gain[1, 0], qk_gain[1, 1]))
    return (jnp.stack(tails), jnp.stack(heads))
```

```python
import functools

import jax
import jax.numpy as jnp
from jax import lax
from jax.experimental import pallas as pl
from jax.experimental.pallas import tpu as pltpu
from jax.sharding import PartitionSpec as P

QH = 6
KVH = 2
HD = 128


def passed_along(x, axis, by):
    peers = lax.axis_size(axis)
    return lax.ppermute(x, axis, [(i, (i + by) % peers) for i in range(peers)])


def qk_normal(values, gain_row):
    factor = lax.rsqrt(jnp.mean(values * values, axis=-1, keepdims=True) + 1e-06)
    return (values * factor * gain_row).astype(jnp.bfloat16)


def fetch_weights(joined_w, output_w):
    return (
        lax.all_gather(joined_w, ("section", "ctx"), axis=0, tiled=True),
        lax.all_gather(output_w, ("section", "ctx"), axis=0, tiled=True),
    )


def attend(inputs, joined_w, output_w, gain_rows, q_gain, k_gain):
    tok_rows = inputs.shape[0]
    groups = QH // KVH
    q_width = QH * HD
    k_width = KVH * HD
    score_scale = float(HD) ** (-0.5)
    widened = inputs.astype(jnp.float32)
    factor = lax.rsqrt(jnp.mean(widened * widened, axis=-1, keepdims=True) + 1e-06)
    normed = (widened * factor * gain_rows[0]).astype(jnp.bfloat16)
    projected = jnp.dot(normed, joined_w, preferred_element_type=jnp.float32)
    queries = qk_normal(projected[:, :q_width].reshape(tok_rows, KVH, groups, HD), q_gain)
    key_rows = qk_normal(
        projected[:, q_width : q_width + k_width].reshape(tok_rows, KVH, HD), k_gain
    )
    key_rows = key_rows.reshape(tok_rows, k_width)
    val_rows = projected[:, q_width + k_width :].astype(jnp.bfloat16)

    def add_block(running, key_block, val_block):
        scores = (
            jnp.einsum("tkgd,skd->tkgs", queries, key_block, preferred_element_type=jnp.float32)
            * score_scale
        )
        weights = jnp.exp(scores)
        numerator = running[0] + jnp.einsum(
            "tkgs,skd->tkgd",
            weights.astype(jnp.bfloat16),
            val_block,
            preferred_element_type=jnp.float32,
        )
        return (numerator, running[1] + jnp.sum(weights, axis=-1))

    initial = (
        jnp.zeros((tok_rows, KVH, groups, HD), jnp.float32),
        jnp.zeros((tok_rows, KVH, groups), jnp.float32),
    )
    running = initial
    pieces = (
        lax.all_gather(key_rows, "ctx", axis=0, tiled=True),
        lax.all_gather(val_rows, "ctx", axis=0, tiled=True),
    )
    row_count = pieces[0].shape[0]
    key_piece = pieces[0].reshape(row_count, KVH, HD)
    val_piece = pieces[1].reshape(row_count, KVH, HD)
    key_blocks = key_piece.reshape(row_count // 256, 256, KVH, HD)
    val_blocks = val_piece.reshape(row_count // 256, 256, KVH, HD)

    def step_block(state_pair, block_pair):
        return (add_block(state_pair, block_pair[0], block_pair[1]), None)

    running, unused = lax.scan(step_block, running, (key_blocks, val_blocks))
    numerator, denominator = running
    attended = (numerator / denominator[..., None]).astype(jnp.bfloat16).reshape(tok_rows, q_width)
    update = lax.dot_general(
        attended, output_w, (((1,), (1,)), ((), ())), preferred_element_type=jnp.float32
    )
    return (widened + gain_rows[1] * update).astype(jnp.bfloat16)


def per_device(
    latent_state, lead_step, tail_qkv, tail_out, head_qkv, head_out, modulation, qk_gain
):
    section_pos = lax.axis_index("section")
    section_count = lax.axis_size("section")
    lead_now = lax.dynamic_index_in_dim(lead_step, section_pos, 0, keepdims=False)
    sender = jnp.mod(section_pos - 1 + section_count, section_count)
    lead_next = lax.dynamic_index_in_dim(lead_step, sender, 0, keepdims=False) + 1
    tail_rows = lax.dynamic_index_in_dim(modulation[0], lead_now, 1, keepdims=False)
    head_rows = lax.dynamic_index_in_dim(modulation[1], lead_next, 1, keepdims=False)
    tail_weights = fetch_weights(tail_qkv, tail_out)
    tail_new = attend(
        latent_state[0], tail_weights[0], tail_weights[1], tail_rows, qk_gain[0, 0], qk_gain[0, 1]
    )
    arrived = passed_along(tail_new, "section", 1)
    head_weights = fetch_weights(head_qkv, head_out)
    head_new = attend(
        arrived, head_weights[0], head_weights[1], head_rows, qk_gain[1, 0], qk_gain[1, 1]
    )
    return (tail_new[None], head_new[None])


EPS = 1e-06
MESH = pl.DeviceIdType.MESH


def receive_slots(zs):
    names = []
    for piece in range(4):
        names += [(piece, "z", d) for d in range(1, zs)]
        names += [(piece, side, d) for side in "xy" for d in range(zs)]
        names += [(piece, "xd"), (piece, "yd")]
        names += [(piece, "sib", j) for j in range(4)]
    for layer in range(2):
        names += [("kv", layer, d) for d in range(1, zs)]
        names += [("kvs", layer, d) for d in range(zs)]
    names += [("state", j) for j in range(4)]
    return {name: i for i, name in enumerate(names)}


def rollout_kernel(
    zs, lead_ref, x_ref, tq_ref, to_ref, hq_ref, ho_ref, mod_ref, qkg_ref,
    tail_ref, head_ref,
    wtq, wto, whq, who, kvb, qbuf, nbuf, abuf, came, send_sems, recv_sems, own_sems,
):
    slots = receive_slots(zs)
    sec = lax.axis_index("section")
    pos = lax.axis_index("ctx")
    z = pos // 2
    k = pos % 2
    sx = sec + 1 - 2 * (sec % 2)
    sy = (sec + 2) % 4
    sd = (sx + 2) % 4
    nxt = (sec + 1) % 4
    prev = (sec + 3) % 4
    half = zs // 2
    tok = x_ref.shape[1]
    shards = (tq_ref, to_ref, hq_ref, ho_ref)
    full = (wtq, wto, whq, who)
    sibling = (sec, 2 * z + 1 - k)
    x_peer = (sx, pos)
    y_peer = (sy, pos)
    z_peer = [(sec, 2 * ((z + d) % zs) + k) for d in range(zs)]
    z_from = [(z + zs - d) % zs for d in range(zs)]

    sends = []

    def send(src, dst, name, device):
        copy = pltpu.make_async_remote_copy(
            src_ref=src, dst_ref=dst,
            send_sem=send_sems.at[len(sends)], recv_sem=recv_sems.at[slots[name]],
            device_id=device, device_id_type=MESH,
        )
        copy.start()
        sends.append(copy)

    def receive(dst, name):
        pltpu.make_async_remote_copy(
            src_ref=dst, dst_ref=dst,
            send_sem=send_sems.at[0], recv_sem=recv_sems.at[slots[name]],
            device_id=sibling, device_id_type=MESH,
        ).wait_recv()

    own_copies = [
        pltpu.make_async_copy(shards[p], full[p].at[sec, z, k], own_sems.at[p]) for p in range(4)
    ]

    def send_own(p):
        w = full[p]
        for d in range(1, zs):
            send(shards[p], w.at[sec, z, k], (p, "z", d), z_peer[d])
        send(shards[p], w.at[sec, z, k], (p, "x", 0), x_peer)
        send(shards[p], w.at[sec, z, k], (p, "y", 0), y_peer)

    def forward_z(p):
        w = full[p]
        for d in range(1, zs):
            block = w.at[sec, z_from[d], k]
            receive(block, (p, "z", d))
            send(block, block, (p, "x", d), x_peer)
            send(block, block, (p, "y", d), y_peer)
        own_copies[p].wait()
        column = w.at[sec, :, k]
        send(column, column, (p, "sib", 0), sibling)

    def forward_xy(p):
        w = full[p]
        for d in range(zs):
            receive(w.at[sx, z_from[d], k], (p, "x", d))
        part = w.at[sx, pl.ds(0, half), k]
        send(part, part, (p, "yd"), y_peer)
        column = w.at[sx, :, k]
        send(column, column, (p, "sib", 1), sibling)
        for d in range(zs):
            receive(w.at[sy, z_from[d], k], (p, "y", d))
        part = w.at[sy, pl.ds(half, zs - half), k]
        send(part, part, (p, "xd"), x_peer)
        column = w.at[sy, :, k]
        send(column, column, (p, "sib", 2), sibling)

    def finish(p):
        w = full[p]
        receive(w.at[sd, pl.ds(0, half), k], (p, "yd"))
        receive(w.at[sd, pl.ds(half, zs - half), k], (p, "xd"))
        column = w.at[sd, :, k]
        send(column, column, (p, "sib", 3), sibling)
        for j, owner in enumerate((sec, sx, sy, sd)):
            receive(w.at[owner, :, 1 - k], (p, "sib", j))

    barrier = pltpu.get_barrier_semaphore()
    partners = z_peer[1:] + [sibling, x_peer, y_peer, (sd, pos)]
    for device in partners:
        pl.semaphore_signal(barrier, inc=1, device_id=device, device_id_type=MESH)
    for copy in own_copies:
        copy.start()
    pl.semaphore_wait(barrier, len(partners))

    def normalize(rows, gain):
        wide = rows.astype(jnp.float32)
        factor = lax.rsqrt(jnp.mean(wide * wide, axis=-1, keepdims=True) + EPS)
        nbuf[...] = (wide * factor * gain).astype(jnp.bfloat16)

    def project(w, first):
        weights = w[:, :, :, :, first : first + 256].reshape(-1, 256)
        return jnp.dot(nbuf[...], weights, preferred_element_type=jnp.float32)

    def head_normal(values, gain):
        factor = lax.rsqrt(jnp.mean(values * values, axis=-1, keepdims=True) + EPS)
        return (values * factor * gain).astype(jnp.bfloat16)

    def keys_values(w, layer):
        k_gain = qkg_ref[layer, pl.ds(1, 1), :]
        keys = project(w, QH * HD)
        block = kvb.at[layer, z, k]
        for h in range(KVH):
            block[:, h * HD : (h + 1) * HD] = head_normal(keys[:, h * HD : (h + 1) * HD], k_gain)
        block[:, KVH * HD :] = project(w, (QH + KVH) * HD).astype(jnp.bfloat16)
        for d in range(1, zs):
            send(block, block, ("kv", layer, d), z_peer[d])
        send(block, block, ("kvs", layer, 0), sibling)

    def queries(w, layer):
        q_gain = qkg_ref[layer, pl.ds(0, 1), :]
        for pair in range(QH // 2):
            both = project(w, pair * 2 * HD)
            for i in range(2):
                h = 2 * pair + i
                row = (h % 3) * tok
                qbuf[h // 3, row : row + tok, :] = head_normal(
                    both[:, i * HD : (i + 1) * HD], q_gain
                )

    def attention(layer):
        num = [None] * KVH
        den = [None] * KVH
        for d in range(zs):
            if d + 1 < zs:
                block = kvb.at[layer, z_from[d + 1], k]
                receive(block, ("kv", layer, d + 1))
                send(block, block, ("kvs", layer, d + 1), sibling)
            receive(kvb.at[layer, z_from[d], 1 - k], ("kvs", layer, d))
            both = kvb[layer, z_from[d]].reshape(2 * tok, 2 * KVH * HD)
            for h in range(KVH):
                scores = lax.dot_general(
                    qbuf[h], both[:, h * HD : (h + 1) * HD], (((1,), (1,)), ((), ())),
                    preferred_element_type=jnp.float32,
                )
                weights = jnp.exp(scores * float(HD) ** (-0.5))
                total = jnp.sum(weights, axis=-1, keepdims=True)
                mixed = jnp.dot(
                    weights.astype(jnp.bfloat16),
                    both[:, (KVH + h) * HD : (KVH + h + 1) * HD],
                    preferred_element_type=jnp.float32,
                )
                num[h] = mixed if d == 0 else num[h] + mixed
                den[h] = total if d == 0 else den[h] + total
        for h in range(KVH):
            result = (num[h] / den[h]).astype(jnp.bfloat16)
            for i in range(3):
                at = (3 * h + i) * HD
                abuf[:, at : at + HD] = result[i * tok : (i + 1) * tok]

    def finish_layer(w, rows_ref, gate, out_ref, after):
        for j in range(4):
            weights = w[j].reshape(-1, QH * HD)
            width = weights.shape[0]
            columns = slice(j * width, (j + 1) * width)
            update = lax.dot_general(
                abuf[...], weights, (((1,), (1,)), ((), ())), preferred_element_type=jnp.float32
            )
            wide = rows_ref[:, columns].astype(jnp.float32)
            out_ref[:, columns] = (wide + gate[:, columns] * update).astype(jnp.bfloat16)
            after(j, columns)

    lead_now = lead_ref[sec]
    lead_next = lead_ref[prev] + 1

    send_own(0)
    send_own(1)
    normalize(x_ref[0], mod_ref[0, 0, pl.ds(lead_now, 1), :])
    forward_z(0)
    send_own(2)
    forward_z(1)
    send_own(3)
    forward_xy(0)
    forward_z(2)
    forward_xy(1)
    finish(0)
    keys_values(wtq, 0)
    queries(wtq, 0)
    forward_z(3)
    forward_xy(2)
    attention(0)
    finish(1)

    def pass_on(j, columns):
        send(tail_ref.at[0, :, columns], came.at[:, columns], ("state", j), (nxt, pos))

    finish_layer(
        wto, x_ref.at[0], mod_ref[0, 1, pl.ds(lead_now, 1), :], tail_ref.at[0], pass_on
    )
    forward_xy(3)
    finish(2)
    for j in range(4):
        width = came.shape[1] // 4
        receive(came.at[:, pl.ds(j * width, width)], ("state", j))
    normalize(came[...], mod_ref[1, 0, pl.ds(lead_next, 1), :])
    keys_values(whq, 1)
    queries(whq, 1)
    finish(3)
    attention(1)
    finish_layer(
        who, came, mod_ref[1, 1, pl.ds(lead_next, 1), :], head_ref.at[0], lambda j, columns: None
    )
    for copy in sends:
        copy.wait_send()


def fused(latent_state, lead_step, tail_qkv, tail_out, head_qkv, head_out, modulation, qk_gain):
    ctx = lax.axis_size("ctx")
    zs = ctx // 2
    rows = tail_qkv.shape[0]
    tok = latent_state.shape[1]
    wide = latent_state.shape[2]
    joined = tail_qkv.shape[1]
    inner = tail_out.shape[1]
    n_slots = len(receive_slots(zs))
    vmem = pl.BlockSpec(memory_space=pltpu.VMEM)
    smem = pl.BlockSpec(memory_space=pltpu.SMEM)
    state = jax.ShapeDtypeStruct(latent_state.shape, jnp.bfloat16)
    return pl.pallas_call(
        functools.partial(rollout_kernel, zs),
        out_shape=(state, state),
        in_specs=[smem] + [vmem] * 7,
        out_specs=(vmem, vmem),
        scratch_shapes=[
            pltpu.VMEM((4, zs, 2, rows, joined), jnp.bfloat16),
            pltpu.VMEM((4, zs, 2, rows, inner), jnp.bfloat16),
            pltpu.VMEM((4, zs, 2, rows, joined), jnp.bfloat16),
            pltpu.VMEM((4, zs, 2, rows, inner), jnp.bfloat16),
            pltpu.VMEM((2, zs, 2, tok, 2 * KVH * HD), jnp.bfloat16),
            pltpu.VMEM((KVH, QH // KVH * tok, HD), jnp.bfloat16),
            pltpu.VMEM((tok, wide), jnp.bfloat16),
            pltpu.VMEM((tok, QH * HD), jnp.bfloat16),
            pltpu.VMEM((tok, wide), jnp.bfloat16),
            pltpu.SemaphoreType.DMA((n_slots,)),
            pltpu.SemaphoreType.DMA((n_slots,)),
            pltpu.SemaphoreType.DMA((4,)),
        ],
        compiler_params=pltpu.CompilerParams(
            collective_id=0, has_side_effects=True, vmem_limit_bytes=48 * 1024 * 1024
        ),
    )(lead_step, latent_state, tail_qkv, tail_out, head_qkv, head_out, modulation, qk_gain)


def solution(mesh):
    in_specs = (
        P("section", "ctx", None),
        P(),
        P(("section", "ctx"), None),
        P(("section", "ctx"), None),
        P(("section", "ctx"), None),
        P(("section", "ctx"), None),
        P(),
        P(),
    )
    out_specs = (P("section", "ctx", None), P("section", "ctx", None))
    planar = mesh.shape["section"] == 4 and mesh.shape["ctx"] == 8
    return jax.shard_map(
        fused if planar else per_device, mesh=mesh, in_specs=in_specs, out_specs=out_specs, check_vma=False
    )
```

```python
import functools

import jax
import jax.numpy as jnp
from jax import lax
from jax.experimental import pallas as pl
from jax.experimental.pallas import tpu as pltpu
from jax.sharding import PartitionSpec as P

QH = 6
KVH = 2
HD = 128


def passed_along(x, axis, by):
    peers = lax.axis_size(axis)
    return lax.ppermute(x, axis, [(i, (i + by) % peers) for i in range(peers)])


def qk_normal(values, gain_row):
    factor = lax.rsqrt(jnp.mean(values * values, axis=-1, keepdims=True) + 1e-06)
    return (values * factor * gain_row).astype(jnp.bfloat16)


def fetch_weights(joined_w, output_w):
    return (
        lax.all_gather(joined_w, ("section", "ctx"), axis=0, tiled=True),
        lax.all_gather(output_w, ("section", "ctx"), axis=0, tiled=True),
    )


def attend(inputs, joined_w, output_w, gain_rows, q_gain, k_gain):
    tok_rows = inputs.shape[0]
    groups = QH // KVH
    q_width = QH * HD
    k_width = KVH * HD
    score_scale = float(HD) ** (-0.5)
    widened = inputs.astype(jnp.float32)
    factor = lax.rsqrt(jnp.mean(widened * widened, axis=-1, keepdims=True) + 1e-06)
    normed = (widened * factor * gain_rows[0]).astype(jnp.bfloat16)
    projected = jnp.dot(normed, joined_w, preferred_element_type=jnp.float32)
    queries = qk_normal(projected[:, :q_width].reshape(tok_rows, KVH, groups, HD), q_gain)
    key_rows = qk_normal(
        projected[:, q_width : q_width + k_width].reshape(tok_rows, KVH, HD), k_gain
    )
    key_rows = key_rows.reshape(tok_rows, k_width)
    val_rows = projected[:, q_width + k_width :].astype(jnp.bfloat16)

    def add_block(running, key_block, val_block):
        scores = (
            jnp.einsum("tkgd,skd->tkgs", queries, key_block, preferred_element_type=jnp.float32)
            * score_scale
        )
        weights = jnp.exp(scores)
        numerator = running[0] + jnp.einsum(
            "tkgs,skd->tkgd",
            weights.astype(jnp.bfloat16),
            val_block,
            preferred_element_type=jnp.float32,
        )
        return (numerator, running[1] + jnp.sum(weights, axis=-1))

    initial = (
        jnp.zeros((tok_rows, KVH, groups, HD), jnp.float32),
        jnp.zeros((tok_rows, KVH, groups), jnp.float32),
    )
    running = initial
    pieces = (
        lax.all_gather(key_rows, "ctx", axis=0, tiled=True),
        lax.all_gather(val_rows, "ctx", axis=0, tiled=True),
    )
    row_count = pieces[0].shape[0]
    key_piece = pieces[0].reshape(row_count, KVH, HD)
    val_piece = pieces[1].reshape(row_count, KVH, HD)
    key_blocks = key_piece.reshape(row_count // 256, 256, KVH, HD)
    val_blocks = val_piece.reshape(row_count // 256, 256, KVH, HD)

    def step_block(state_pair, block_pair):
        return (add_block(state_pair, block_pair[0], block_pair[1]), None)

    running, unused = lax.scan(step_block, running, (key_blocks, val_blocks))
    numerator, denominator = running
    attended = (numerator / denominator[..., None]).astype(jnp.bfloat16).reshape(tok_rows, q_width)
    update = lax.dot_general(
        attended, output_w, (((1,), (1,)), ((), ())), preferred_element_type=jnp.float32
    )
    return (widened + gain_rows[1] * update).astype(jnp.bfloat16)


def per_device(
    latent_state, lead_step, tail_qkv, tail_out, head_qkv, head_out, modulation, qk_gain
):
    section_pos = lax.axis_index("section")
    section_count = lax.axis_size("section")
    lead_now = lax.dynamic_index_in_dim(lead_step, section_pos, 0, keepdims=False)
    sender = jnp.mod(section_pos - 1 + section_count, section_count)
    lead_next = lax.dynamic_index_in_dim(lead_step, sender, 0, keepdims=False) + 1
    tail_rows = lax.dynamic_index_in_dim(modulation[0], lead_now, 1, keepdims=False)
    head_rows = lax.dynamic_index_in_dim(modulation[1], lead_next, 1, keepdims=False)
    tail_weights = fetch_weights(tail_qkv, tail_out)
    tail_new = attend(
        latent_state[0], tail_weights[0], tail_weights[1], tail_rows, qk_gain[0, 0], qk_gain[0, 1]
    )
    arrived = passed_along(tail_new, "section", 1)
    head_weights = fetch_weights(head_qkv, head_out)
    head_new = attend(
        arrived, head_weights[0], head_weights[1], head_rows, qk_gain[1, 0], qk_gain[1, 1]
    )
    return (tail_new[None], head_new[None])


EPS = 1e-06
MESH = pl.DeviceIdType.MESH


def receive_slots(zs):
    names = []
    for piece in range(4):
        names += [(piece, side, d) for side in "xy" for d in range(zs)]
        names += [(piece, "xd"), (piece, "yd")]
        names += [(piece, "sib", j) for j in range(4)]
    for layer in range(2):
        names += [("kvs", layer, d) for d in range(zs)]
    names += [("state",)] + [("attended", h) for h in range(KVH)]
    return {name: i for i, name in enumerate(names)}


def rollout_kernel(
    zs, lead_ref, x_hbm, tq_ref, to_ref, hq_ref, ho_ref, mod_hbm, qkg_hbm,
    tail_ref, head_ref,
    wtq, wto, whq, who, kvb, qbuf, nbuf, abuf, afar, came, x_ref, mod_ref, qkg_ref,
    send_sems, recv_sems, z_sems, own_sems,
):
    slots = receive_slots(zs)
    sec = lax.axis_index("section")
    pos = lax.axis_index("ctx")
    z = pos // 2
    k = pos % 2
    sx = sec + 1 - 2 * (sec % 2)
    sy = (sec + 2) % 4
    sd = (sx + 2) % 4
    nxt = (sec + 1) % 4
    prev = (sec + 3) % 4
    half = zs // 2
    tok = x_ref.shape[1]
    shards = (tq_ref, to_ref, hq_ref, ho_ref)
    full = (wtq, wto, whq, who)
    sibling = (sec, 2 * z + 1 - k)
    x_peer = (sx, pos)
    y_peer = (sy, pos)
    z_up = (sec, 2 * ((z + 1) % zs) + k)
    z_down = (sec, 2 * ((z + zs - 1) % zs) + k)
    z_from = [z, z + 1 - 2 * (z % 2), 2 - z // 2, 3 - 3 * (z // 2)]

    sends = []

    def send(src, dst, name, device):
        copy = pltpu.make_async_remote_copy(
            src_ref=src, dst_ref=dst,
            send_sem=send_sems.at[len(sends)], recv_sem=recv_sems.at[slots[name]],
            device_id=device, device_id_type=MESH,
        )
        copy.start()
        sends.append((None, copy.wait_send))

    def send_z(src, dst, row, owner, up):
        slot = len(sends)
        goes = (owner <= z) & (z < zs - 1) if up else (owner >= z) & (z > 0)

        def copy():
            return pltpu.make_async_remote_copy(
                src_ref=src, dst_ref=dst,
                send_sem=send_sems.at[slot], recv_sem=z_sems.at[row, owner],
                device_id=z_up if up else z_down, device_id_type=MESH,
            )

        @pl.when(goes)
        def _():
            copy().start()

        sends.append((goes, lambda: copy().wait_send()))

    def receive_z(dst, row, owner):
        pltpu.make_async_remote_copy(
            src_ref=dst, dst_ref=dst,
            send_sem=send_sems.at[0], recv_sem=z_sems.at[row, owner],
            device_id=sibling, device_id_type=MESH,
        ).wait_recv()

    def receive(dst, name):
        pltpu.make_async_remote_copy(
            src_ref=dst, dst_ref=dst,
            send_sem=send_sems.at[0], recv_sem=recv_sems.at[slots[name]],
            device_id=sibling, device_id_type=MESH,
        ).wait_recv()

    own_copies = [
        pltpu.make_async_copy(shards[p], full[p].at[sec, z, k], own_sems.at[p]) for p in range(4)
    ]

    def send_own(p):
        w = full[p]
        for up in (True, False):
            send_z(shards[p], w.at[sec, z, k], p, z, up)
        send(shards[p], w.at[sec, z, k], (p, "x", 0), x_peer)
        send(shards[p], w.at[sec, z, k], (p, "y", 0), y_peer)

    def forward_z(p):
        w = full[p]
        for d in range(1, zs):
            block = w.at[sec, z_from[d], k]
            receive_z(block, p, z_from[d])
            for up in (True, False):
                send_z(block, block, p, z_from[d], up)
            send(block, block, (p, "x", d), x_peer)
            send(block, block, (p, "y", d), y_peer)
        own_copies[p].wait()
        column = w.at[sec, :, k]
        send(column, column, (p, "sib", 0), sibling)

    def forward_xy(p):
        w = full[p]
        for d in range(zs):
            receive(w.at[sx, z_from[d], k], (p, "x", d))
        part = w.at[sx, pl.ds(0, half), k]
        send(part, part, (p, "yd"), y_peer)
        column = w.at[sx, :, k]
        send(column, column, (p, "sib", 1), sibling)
        for d in range(zs):
            receive(w.at[sy, z_from[d], k], (p, "y", d))
        part = w.at[sy, pl.ds(half, zs - half), k]
        send(part, part, (p, "xd"), x_peer)
        column = w.at[sy, :, k]
        send(column, column, (p, "sib", 2), sibling)

    def finish(p):
        w = full[p]
        receive(w.at[sd, pl.ds(0, half), k], (p, "yd"))
        receive(w.at[sd, pl.ds(half, zs - half), k], (p, "xd"))
        column = w.at[sd, :, k]
        send(column, column, (p, "sib", 3), sibling)
        for j, owner in enumerate((sec, sx, sy, sd)):
            receive(w.at[owner, :, 1 - k], (p, "sib", j))

    barrier = pltpu.get_barrier_semaphore()
    partners = [z_up, z_down, sibling, x_peer, y_peer, (sd, pos)]
    for device in partners:
        pl.semaphore_signal(barrier, inc=1, device_id=device, device_id_type=MESH)
    small_copies = [
        pltpu.make_async_copy(src, dst, own_sems.at[4 + i])
        for i, (src, dst) in enumerate(((x_hbm, x_ref), (mod_hbm, mod_ref), (qkg_hbm, qkg_ref)))
    ]
    for copy in small_copies + own_copies:
        copy.start()
    pl.semaphore_wait(barrier, len(partners))

    def normalize(rows, gain):
        wide = rows.astype(jnp.float32)
        factor = lax.rsqrt(jnp.mean(wide * wide, axis=-1, keepdims=True) + EPS)
        nbuf[...] = (wide * factor * gain).astype(jnp.bfloat16)

    def project(w, first):
        weights = w[:, :, :, :, first : first + 256].reshape(-1, 256)
        return jnp.dot(nbuf[...], weights, preferred_element_type=jnp.float32)

    def head_normal(values, gain):
        factor = lax.rsqrt(jnp.mean(values * values, axis=-1, keepdims=True) + EPS)
        return (values * factor * gain).astype(jnp.bfloat16)

    def keys_values(w, layer):
        k_gain = qkg_ref[layer, pl.ds(1, 1), :]
        keys = project(w, QH * HD)
        block = kvb.at[layer, z, k]
        for h in range(KVH):
            block[:, h * HD : (h + 1) * HD] = head_normal(keys[:, h * HD : (h + 1) * HD], k_gain)
        block[:, KVH * HD :] = project(w, (QH + KVH) * HD).astype(jnp.bfloat16)
        for up in (True, False):
            send_z(block, block, 4 + layer, z, up)
        send(block, block, ("kvs", layer, 0), sibling)

    def queries(w, layer):
        q_gain = qkg_ref[layer, pl.ds(0, 1), :]
        for pair in range(QH // 2):
            both = project(w, pair * 2 * HD)
            for i in range(2):
                h = 2 * pair + i
                row = (h % 3) * tok
                qbuf[h // 3, row : row + tok, :] = head_normal(
                    both[:, i * HD : (i + 1) * HD], q_gain
                )

    def attention(layer, after):
        num = [None] * KVH
        den = [None] * KVH
        for d in range(zs):
            if d + 1 < zs:
                block = kvb.at[layer, z_from[d + 1], k]
                receive_z(block, 4 + layer, z_from[d + 1])
                for up in (True, False):
                    send_z(block, block, 4 + layer, z_from[d + 1], up)
                send(block, block, ("kvs", layer, d + 1), sibling)
            receive(kvb.at[layer, z_from[d], 1 - k], ("kvs", layer, d))
            both = kvb[layer, z_from[d]].reshape(2 * tok, 2 * KVH * HD)
            for h in range(KVH):
                scores = lax.dot_general(
                    qbuf[h], both[:, h * HD : (h + 1) * HD], (((1,), (1,)), ((), ())),
                    preferred_element_type=jnp.float32,
                )
                weights = jnp.exp(scores * float(HD) ** (-0.5))
                total = jnp.sum(weights, axis=-1, keepdims=True)
                mixed = jnp.dot(
                    weights.astype(jnp.bfloat16),
                    both[:, (KVH + h) * HD : (KVH + h + 1) * HD],
                    preferred_element_type=jnp.float32,
                )
                num[h] = mixed if d == 0 else num[h] + mixed
                den[h] = total if d == 0 else den[h] + total
                if d == zs - 1:
                    result = (num[h] / den[h]).astype(jnp.bfloat16)
                    for i in range(3):
                        abuf[layer, h, :, i * HD : (i + 1) * HD] = result[i * tok : (i + 1) * tok]
                    after(h)

    def finish_layer(w, attended_ref, rows_ref, gate, out_ref):
        for j in range(4):
            weights = w[j].reshape(-1, QH * HD)
            width = weights.shape[0]
            columns = slice(j * width, (j + 1) * width)
            part = weights.shape[1] // KVH
            update = sum(
                lax.dot_general(
                    attended_ref[h], weights[:, h * part : (h + 1) * part],
                    (((1,), (1,)), ((), ())), preferred_element_type=jnp.float32,
                )
                for h in range(KVH)
            )
            wide = rows_ref[:, columns].astype(jnp.float32)
            out_ref[:, columns] = (wide + gate[:, columns] * update).astype(jnp.bfloat16)

    lead_now = lead_ref[sec]
    lead_came = lead_ref[prev]

    send_own(0)
    for copy in small_copies:
        copy.wait()
    normalize(x_ref[0], mod_ref[0, 0, pl.ds(lead_now, 1), :])
    forward_z(0)
    send_own(1)
    forward_xy(0)
    forward_z(1)
    send_own(2)
    finish(0)
    keys_values(wtq, 0)
    forward_z(2)
    queries(wtq, 0)
    forward_xy(1)
    attention(0, lambda h: None)
    send_own(3)
    finish(1)
    finish_layer(wto, abuf.at[0], x_ref.at[0], mod_ref[0, 1, pl.ds(lead_now, 1), :], tail_ref.at[0])
    forward_xy(2)
    forward_z(3)
    send(tail_ref.at[0], came, ("state",), (nxt, pos))
    normalize(tail_ref[0], mod_ref[1, 0, pl.ds(lead_now + 1, 1), :])
    finish(2)
    keys_values(whq, 1)
    queries(whq, 1)
    forward_xy(3)
    attention(1, lambda h: send(abuf.at[1, h], afar.at[h], ("attended", h), (nxt, pos)))
    finish(3)
    receive(came, ("state",))
    for h in range(KVH):
        receive(afar.at[h], ("attended", h))
    finish_layer(who, afar, came, mod_ref[1, 1, pl.ds(lead_came + 1, 1), :], head_ref.at[0])
    for goes, wait in sends:
        if goes is None:
            wait()
        else:
            pl.when(goes)(wait)


def fused(latent_state, lead_step, tail_qkv, tail_out, head_qkv, head_out, modulation, qk_gain):
    ctx = lax.axis_size("ctx")
    zs = ctx // 2
    rows = tail_qkv.shape[0]
    tok = latent_state.shape[1]
    wide = latent_state.shape[2]
    joined = tail_qkv.shape[1]
    inner = tail_out.shape[1]
    n_slots = len(receive_slots(zs))
    vmem = pl.BlockSpec(memory_space=pltpu.VMEM)
    smem = pl.BlockSpec(memory_space=pltpu.SMEM)
    state = jax.ShapeDtypeStruct(latent_state.shape, jnp.bfloat16)
    return pl.pallas_call(
        functools.partial(rollout_kernel, zs),
        out_shape=(state, state),
        in_specs=[smem] + [pl.BlockSpec(memory_space=pltpu.HBM)] * 7,
        out_specs=(vmem, vmem),
        scratch_shapes=[
            pltpu.VMEM((4, zs, 2, rows, joined), jnp.bfloat16),
            pltpu.VMEM((4, zs, 2, rows, inner), jnp.bfloat16),
            pltpu.VMEM((4, zs, 2, rows, joined), jnp.bfloat16),
            pltpu.VMEM((4, zs, 2, rows, inner), jnp.bfloat16),
            pltpu.VMEM((2, zs, 2, tok, 2 * KVH * HD), jnp.bfloat16),
            pltpu.VMEM((KVH, QH // KVH * tok, HD), jnp.bfloat16),
            pltpu.VMEM((tok, wide), jnp.bfloat16),
            pltpu.VMEM((2, KVH, tok, QH // KVH * HD), jnp.bfloat16),
            pltpu.VMEM((KVH, tok, QH // KVH * HD), jnp.bfloat16),
            pltpu.VMEM((tok, wide), jnp.bfloat16),
            pltpu.VMEM(latent_state.shape, jnp.bfloat16),
            pltpu.VMEM(modulation.shape, jnp.float32),
            pltpu.VMEM(qk_gain.shape, jnp.float32),
            pltpu.SemaphoreType.DMA((n_slots + 6 * 2 * zs,)),
            pltpu.SemaphoreType.DMA((n_slots,)),
            pltpu.SemaphoreType.DMA((6, zs)),
            pltpu.SemaphoreType.DMA((7,)),
        ],
        compiler_params=pltpu.CompilerParams(
            collective_id=0, has_side_effects=True, vmem_limit_bytes=48 * 1024 * 1024
        ),
    )(lead_step, latent_state, tail_qkv, tail_out, head_qkv, head_out, modulation, qk_gain)


def solution(mesh):
    in_specs = (
        P("section", "ctx", None),
        P(),
        P(("section", "ctx"), None),
        P(("section", "ctx"), None),
        P(("section", "ctx"), None),
        P(("section", "ctx"), None),
        P(),
        P(),
    )
    out_specs = (P("section", "ctx", None), P("section", "ctx", None))
    planar = mesh.shape["section"] == 4 and mesh.shape["ctx"] == 8
    return jax.shard_map(
        fused if planar else per_device, mesh=mesh, in_specs=in_specs, out_specs=out_specs, check_vma=False
    )
```

```python
import functools

import jax
import jax.numpy as jnp
from jax import lax
from jax.experimental import pallas as pl
from jax.experimental.pallas import tpu as pltpu
from jax.sharding import PartitionSpec as P

QH = 6
KVH = 2
HD = 128


def passed_along(x, axis, by):
    peers = lax.axis_size(axis)
    return lax.ppermute(x, axis, [(i, (i + by) % peers) for i in range(peers)])


def qk_normal(values, gain_row):
    factor = lax.rsqrt(jnp.mean(values * values, axis=-1, keepdims=True) + 1e-06)
    return (values * factor * gain_row).astype(jnp.bfloat16)


def fetch_weights(joined_w, output_w):
    return (
        lax.all_gather(joined_w, ("section", "ctx"), axis=0, tiled=True),
        lax.all_gather(output_w, ("section", "ctx"), axis=0, tiled=True),
    )


def attend(inputs, joined_w, output_w, gain_rows, q_gain, k_gain):
    tok_rows = inputs.shape[0]
    groups = QH // KVH
    q_width = QH * HD
    k_width = KVH * HD
    score_scale = float(HD) ** (-0.5)
    widened = inputs.astype(jnp.float32)
    factor = lax.rsqrt(jnp.mean(widened * widened, axis=-1, keepdims=True) + 1e-06)
    normed = (widened * factor * gain_rows[0]).astype(jnp.bfloat16)
    projected = jnp.dot(normed, joined_w, preferred_element_type=jnp.float32)
    queries = qk_normal(projected[:, :q_width].reshape(tok_rows, KVH, groups, HD), q_gain)
    key_rows = qk_normal(
        projected[:, q_width : q_width + k_width].reshape(tok_rows, KVH, HD), k_gain
    )
    key_rows = key_rows.reshape(tok_rows, k_width)
    val_rows = projected[:, q_width + k_width :].astype(jnp.bfloat16)

    def add_block(running, key_block, val_block):
        scores = (
            jnp.einsum("tkgd,skd->tkgs", queries, key_block, preferred_element_type=jnp.float32)
            * score_scale
        )
        weights = jnp.exp(scores)
        numerator = running[0] + jnp.einsum(
            "tkgs,skd->tkgd",
            weights.astype(jnp.bfloat16),
            val_block,
            preferred_element_type=jnp.float32,
        )
        return (numerator, running[1] + jnp.sum(weights, axis=-1))

    initial = (
        jnp.zeros((tok_rows, KVH, groups, HD), jnp.float32),
        jnp.zeros((tok_rows, KVH, groups), jnp.float32),
    )
    running = initial
    pieces = (
        lax.all_gather(key_rows, "ctx", axis=0, tiled=True),
        lax.all_gather(val_rows, "ctx", axis=0, tiled=True),
    )
    row_count = pieces[0].shape[0]
    key_piece = pieces[0].reshape(row_count, KVH, HD)
    val_piece = pieces[1].reshape(row_count, KVH, HD)
    key_blocks = key_piece.reshape(row_count // 256, 256, KVH, HD)
    val_blocks = val_piece.reshape(row_count // 256, 256, KVH, HD)

    def step_block(state_pair, block_pair):
        return (add_block(state_pair, block_pair[0], block_pair[1]), None)

    running, unused = lax.scan(step_block, running, (key_blocks, val_blocks))
    numerator, denominator = running
    attended = (numerator / denominator[..., None]).astype(jnp.bfloat16).reshape(tok_rows, q_width)
    update = lax.dot_general(
        attended, output_w, (((1,), (1,)), ((), ())), preferred_element_type=jnp.float32
    )
    return (widened + gain_rows[1] * update).astype(jnp.bfloat16)


def per_device(
    latent_state, lead_step, tail_qkv, tail_out, head_qkv, head_out, modulation, qk_gain
):
    section_pos = lax.axis_index("section")
    section_count = lax.axis_size("section")
    lead_now = lax.dynamic_index_in_dim(lead_step, section_pos, 0, keepdims=False)
    sender = jnp.mod(section_pos - 1 + section_count, section_count)
    lead_next = lax.dynamic_index_in_dim(lead_step, sender, 0, keepdims=False) + 1
    tail_rows = lax.dynamic_index_in_dim(modulation[0], lead_now, 1, keepdims=False)
    head_rows = lax.dynamic_index_in_dim(modulation[1], lead_next, 1, keepdims=False)
    tail_weights = fetch_weights(tail_qkv, tail_out)
    tail_new = attend(
        latent_state[0], tail_weights[0], tail_weights[1], tail_rows, qk_gain[0, 0], qk_gain[0, 1]
    )
    arrived = passed_along(tail_new, "section", 1)
    head_weights = fetch_weights(head_qkv, head_out)
    head_new = attend(
        arrived, head_weights[0], head_weights[1], head_rows, qk_gain[1, 0], qk_gain[1, 1]
    )
    return (tail_new[None], head_new[None])


EPS = 1e-06
MESH = pl.DeviceIdType.MESH


def receive_slots(zs):
    names = []
    for piece in range(4):
        names += [(piece, "swap", i) for i in range(3)]
        names += [(piece, side, d) for side in "xy" for d in range(zs)]
        names += [(piece, "xd"), (piece, "yd")]
    for layer in range(2):
        names += [("normed", layer)] + [("part", layer, j) for j in range(4)]
    names += [("state",)] + [("attended",)]
    return {name: i for i, name in enumerate(names)}


def rollout_kernel(
    zs, lead_ref, x_hbm, tq_ref, to_ref, hq_ref, ho_ref, mod_hbm, qkg_hbm,
    tail_ref, head_ref,
    wtq, wto, whq, who, kvb, qbuf, nbuf, abuf, afar, part, got, came, num, den, x_ref, mod_ref, qkg_ref,
    send_sems, recv_sems, z_sems, own_sems,
):
    slots = receive_slots(zs)
    sec = lax.axis_index("section")
    pos = lax.axis_index("ctx")
    z = pos // 2
    k = pos % 2
    sx = sec + 1 - 2 * (sec % 2)
    sy = (sec + 2) % 4
    sd = (sx + 2) % 4
    nxt = (sec + 1) % 4
    prev = (sec + 3) % 4
    half = zs // 2
    tok = x_ref.shape[1]
    groups = QH // KVH
    q_part = groups * HD
    shards = (tq_ref, to_ref, hq_ref, ho_ref)
    full = (wtq, wto, whq, who)
    sibling = (sec, 2 * z + 1 - k)
    x_peer = (sx, pos)
    y_peer = (sy, pos)
    z_up = (sec, 2 * ((z + 1) % zs) + k)
    z_down = (sec, 2 * ((z + zs - 1) % zs) + k)
    z_from = [z, z + 1 - 2 * (z % 2), 2 - z // 2, 3 - 3 * (z // 2)]

    sends = []

    def send(src, dst, name, device):
        copy = pltpu.make_async_remote_copy(
            src_ref=src, dst_ref=dst,
            send_sem=send_sems.at[len(sends)], recv_sem=recv_sems.at[slots[name]],
            device_id=device, device_id_type=MESH,
        )
        copy.start()
        sends.append((None, copy.wait_send))

    def send_z(block, row, owner, up):
        slot = len(sends)
        goes = (owner <= z) & (z < zs - 1) if up else (owner >= z) & (z > 0)

        def copy():
            return pltpu.make_async_remote_copy(
                src_ref=block, dst_ref=block,
                send_sem=send_sems.at[slot], recv_sem=z_sems.at[row, owner],
                device_id=z_up if up else z_down, device_id_type=MESH,
            )

        @pl.when(goes)
        def _():
            copy().start()

        sends.append((goes, lambda: copy().wait_send()))

    def receive(dst, name):
        pltpu.make_async_remote_copy(
            src_ref=dst, dst_ref=dst,
            send_sem=send_sems.at[0], recv_sem=recv_sems.at[slots[name]],
            device_id=sibling, device_id_type=MESH,
        ).wait_recv()

    def receive_z(dst, row, owner):
        pltpu.make_async_remote_copy(
            src_ref=dst, dst_ref=dst,
            send_sem=send_sems.at[0], recv_sem=z_sems.at[row, owner],
            device_id=sibling, device_id_type=MESH,
        ).wait_recv()

    def head_columns(p, core):
        starts = [(core * q_part, 0, q_part)]
        if p % 2 == 0:
            starts += [
                (QH * HD + core * HD, q_part, HD),
                ((QH + KVH) * HD + core * HD, q_part + HD, HD),
            ]
        return [(pl.multiple_of(at, HD), to, width) for at, to, width in starts]

    own_copies = [
        [
            pltpu.make_async_copy(
                shards[p].at[:, pl.ds(at, width)],
                full[p].at[sec, z, k, :, pl.ds(to, width)],
                own_sems.at[3 * p + i],
            )
            for i, (at, to, width) in enumerate(head_columns(p, k))
        ]
        for p in range(4)
    ]

    def swap(p):
        for i, (at, to, width) in enumerate(head_columns(p, 1 - k)):
            send(
                shards[p].at[:, pl.ds(at, width)],
                full[p].at[sec, z, k, :, pl.ds(to, width)], (p, "swap", i), sibling,
            )

    def send_own(p):
        w = full[p]
        for copy in own_copies[p]:
            copy.wait()
        for i, (at, to, width) in enumerate(head_columns(p, k)):
            receive(w.at[sec, z, 1 - k, :, pl.ds(to, width)], (p, "swap", i))
        block = w.at[sec, z]
        for up in (True, False):
            send_z(block, p, z, up)
        send(block, block, (p, "x", 0), x_peer)
        send(block, block, (p, "y", 0), y_peer)

    def forward_z(p):
        w = full[p]
        for d in range(1, zs):
            block = w.at[sec, z_from[d]]
            receive_z(block, p, z_from[d])
            for up in (True, False):
                send_z(block, p, z_from[d], up)
            send(block, block, (p, "x", d), x_peer)
            send(block, block, (p, "y", d), y_peer)

    def forward_xy(p):
        w = full[p]
        for d in range(zs):
            receive(w.at[sx, z_from[d]], (p, "x", d))
        block = w.at[sx, pl.ds(0, half)]
        send(block, block, (p, "yd"), y_peer)
        for d in range(zs):
            receive(w.at[sy, z_from[d]], (p, "y", d))
        block = w.at[sy, pl.ds(half, zs - half)]
        send(block, block, (p, "xd"), x_peer)

    def finish(p):
        w = full[p]
        receive(w.at[sd, pl.ds(0, half)], (p, "yd"))
        receive(w.at[sd, pl.ds(half, zs - half)], (p, "xd"))

    barrier = pltpu.get_barrier_semaphore()
    partners = [z_up, z_down, sibling, x_peer, y_peer, (sd, pos)]
    for device in partners:
        pl.semaphore_signal(barrier, inc=1, device_id=device, device_id_type=MESH)
    small_copies = [
        pltpu.make_async_copy(src, dst, own_sems.at[12 + i])
        for i, (src, dst) in enumerate(((x_hbm, x_ref), (mod_hbm, mod_ref), (qkg_hbm, qkg_ref)))
    ]
    for copies in own_copies[:1] + [small_copies] + own_copies[1:]:
        for copy in copies:
            copy.start()
    pl.semaphore_wait(barrier, len(partners))

    def normalize(layer, rows, gain):
        wide = rows.astype(jnp.float32)
        factor = lax.rsqrt(jnp.mean(wide * wide, axis=-1, keepdims=True) + EPS)
        block = nbuf.at[layer, k]
        block[...] = (wide * factor * gain).astype(jnp.bfloat16)
        send(block, block, ("normed", layer), sibling)

    def project(w, layer, first, width):
        weights = w[:, :, :, :, first : first + width].reshape(-1, width)
        rows = nbuf[layer].reshape(2 * tok, -1)
        return jnp.dot(rows, weights, preferred_element_type=jnp.float32)

    def head_normal(values, gain):
        factor = lax.rsqrt(jnp.mean(values * values, axis=-1, keepdims=True) + EPS)
        return (values * factor * gain).astype(jnp.bfloat16)

    def keys_values(w, layer):
        receive(nbuf.at[layer, 1 - k], ("normed", layer))
        both = project(w, layer, q_part, 2 * HD)
        block = kvb.at[layer, z]
        block[:, :HD] = head_normal(both[:, :HD], qkg_ref[layer, pl.ds(1, 1), :])
        block[:, HD:] = both[:, HD:].astype(jnp.bfloat16)
        for up in (True, False):
            send_z(block, 4 + layer, z, up)

    def queries(w, layer):
        gain = qkg_ref[layer, pl.ds(0, 1), :]
        values = project(w, layer, 0, q_part)
        for i in range(groups):
            qbuf[i] = head_normal(values[:, i * HD : (i + 1) * HD], gain)

    def attention(layer):
        for d in range(zs):
            if d + 1 < zs:
                block = kvb.at[layer, z_from[d + 1]]
                receive_z(block, 4 + layer, z_from[d + 1])
                for up in (True, False):
                    send_z(block, 4 + layer, z_from[d + 1], up)

            @pl.loop(0, groups)
            def _(i):
                keys = kvb[layer, z_from[d], :, :HD]
                values = kvb[layer, z_from[d], :, HD:]
                scores = lax.dot_general(
                    qbuf[i], keys, (((1,), (1,)), ((), ())), preferred_element_type=jnp.float32
                )
                weights = jnp.exp(scores * float(HD) ** (-0.5))
                total = jnp.sum(weights, axis=-1, keepdims=True)
                mixed = jnp.dot(
                    weights.astype(jnp.bfloat16), values, preferred_element_type=jnp.float32
                )
                if d > 0:
                    total = total + den[i]
                    mixed = mixed + num[i]
                if d < zs - 1:
                    den[i] = total
                    num[i] = mixed
                else:
                    abuf[layer, i] = (mixed / total).astype(jnp.bfloat16)

    def finish_layer(w, layer, attended_ref, rows_ref, gate, out_ref):
        rows = jnp.concatenate([attended_ref[i] for i in range(groups)], axis=1)
        width = rows_ref.shape[1] // 4
        for j in range(4):
            columns = slice(j * width, (j + 1) * width)
            update = lax.dot_general(
                rows, w[j].reshape(width, q_part),
                (((1,), (1,)), ((), ())), preferred_element_type=jnp.float32,
            )
            part[layer, 0, :, columns] = update[:tok]
            part[layer, 1, :, columns] = update[tok:]
            send(
                part.at[layer, 1 - k, :, columns], got.at[layer, :, columns],
                ("part", layer, j), sibling,
            )
        for j in range(4):
            columns = slice(j * width, (j + 1) * width)
            receive(got.at[layer, :, columns], ("part", layer, j))
            update = part[layer, k, :, columns] + got[layer, :, columns]
            wide = rows_ref[:, columns].astype(jnp.float32)
            out_ref[:, columns] = (wide + gate[:, columns] * update).astype(jnp.bfloat16)

    lead_now = lead_ref[sec]
    lead_came = lead_ref[prev]

    swap(0)
    swap(1)
    send_own(0)
    for copy in small_copies:
        copy.wait()
    normalize(0, x_ref[0], mod_ref[0, lead_now, pl.ds(0, 1), :])
    swap(2)
    swap(3)
    forward_z(0)
    send_own(1)
    forward_xy(0)
    forward_z(1)
    send_own(2)
    finish(0)
    keys_values(wtq, 0)
    forward_z(2)
    queries(wtq, 0)
    forward_xy(1)
    attention(0)
    send_own(3)
    finish(1)
    finish_layer(
        wto, 0, abuf.at[0], x_ref.at[0], mod_ref[0, lead_now, pl.ds(1, 1), :], tail_ref.at[0]
    )
    normalize(1, tail_ref[0], mod_ref[1, lead_now + 1, pl.ds(0, 1), :])
    forward_xy(2)
    forward_z(3)
    send(tail_ref.at[0], came, ("state",), (nxt, pos))
    finish(2)
    keys_values(whq, 1)
    queries(whq, 1)
    forward_xy(3)
    attention(1)
    send(abuf.at[1], afar, ("attended",), (nxt, pos))
    finish(3)
    receive(came, ("state",))
    receive(afar, ("attended",))
    finish_layer(who, 1, afar, came, mod_ref[1, lead_came + 1, pl.ds(1, 1), :], head_ref.at[0])
    for goes, wait in sends:
        if goes is None:
            wait()
        else:
            pl.when(goes)(wait)


def fused(latent_state, lead_step, tail_qkv, tail_out, head_qkv, head_out, modulation, qk_gain):
    zs = lax.axis_size("ctx") // 2
    rows = tail_qkv.shape[0]
    tok = latent_state.shape[1]
    wide = latent_state.shape[2]
    joined = tail_qkv.shape[1] // 2
    inner = tail_out.shape[1] // 2
    groups = QH // KVH
    n_slots = len(receive_slots(zs))
    by_lead = jnp.swapaxes(modulation, 1, 2)
    vmem = pl.BlockSpec(memory_space=pltpu.VMEM)
    smem = pl.BlockSpec(memory_space=pltpu.SMEM)
    state = jax.ShapeDtypeStruct(latent_state.shape, jnp.bfloat16)
    return pl.pallas_call(
        functools.partial(rollout_kernel, zs),
        out_shape=(state, state),
        in_specs=[smem] + [pl.BlockSpec(memory_space=pltpu.HBM)] * 7,
        out_specs=(vmem, vmem),
        scratch_shapes=[
            pltpu.VMEM((4, zs, 2, rows, joined), jnp.bfloat16),
            pltpu.VMEM((4, zs, 2, rows, inner), jnp.bfloat16),
            pltpu.VMEM((4, zs, 2, rows, joined), jnp.bfloat16),
            pltpu.VMEM((4, zs, 2, rows, inner), jnp.bfloat16),
            pltpu.VMEM((2, zs, 2 * tok, 2 * HD), jnp.bfloat16),
            pltpu.VMEM((groups, 2 * tok, HD), jnp.bfloat16),
            pltpu.VMEM((2, 2, tok, wide), jnp.bfloat16),
            pltpu.VMEM((2, groups, 2 * tok, HD), jnp.bfloat16),
            pltpu.VMEM((groups, 2 * tok, HD), jnp.bfloat16),
            pltpu.VMEM((2, 2, tok, wide), jnp.float32),
            pltpu.VMEM((2, tok, wide), jnp.float32),
            pltpu.VMEM((tok, wide), jnp.bfloat16),
            pltpu.VMEM((groups, 2 * tok, HD), jnp.float32),
            pltpu.VMEM((groups, 2 * tok, 1), jnp.float32),
            pltpu.VMEM(latent_state.shape, jnp.bfloat16),
            pltpu.VMEM(by_lead.shape, jnp.float32),
            pltpu.VMEM(qk_gain.shape, jnp.float32),
            pltpu.SemaphoreType.DMA((n_slots + 6 * 2 * zs,)),
            pltpu.SemaphoreType.DMA((n_slots,)),
            pltpu.SemaphoreType.DMA((6, zs)),
            pltpu.SemaphoreType.DMA((15,)),
        ],
        compiler_params=pltpu.CompilerParams(
            collective_id=0, has_side_effects=True, vmem_limit_bytes=48 * 1024 * 1024
        ),
    )(lead_step, latent_state, tail_qkv, tail_out, head_qkv, head_out, by_lead, qk_gain)


def solution(mesh):
    in_specs = (
        P("section", "ctx", None),
        P(),
        P(("section", "ctx"), None),
        P(("section", "ctx"), None),
        P(("section", "ctx"), None),
        P(("section", "ctx"), None),
        P(),
        P(),
    )
    out_specs = (P("section", "ctx", None), P("section", "ctx", None))
    planar = mesh.shape["section"] == 4 and mesh.shape["ctx"] == 8
    return jax.shard_map(
        fused if planar else per_device, mesh=mesh, in_specs=in_specs, out_specs=out_specs, check_vma=False
    )
```

```python
import functools

import jax
import jax.numpy as jnp
from jax import lax
from jax.experimental import pallas as pl
from jax.experimental.pallas import tpu as pltpu
from jax.sharding import PartitionSpec as P

QH = 6
KVH = 2
HD = 128


def passed_along(x, axis, by):
    peers = lax.axis_size(axis)
    return lax.ppermute(x, axis, [(i, (i + by) % peers) for i in range(peers)])


def qk_normal(values, gain_row):
    factor = lax.rsqrt(jnp.mean(values * values, axis=-1, keepdims=True) + 1e-06)
    return (values * factor * gain_row).astype(jnp.bfloat16)


def fetch_weights(joined_w, output_w):
    return (
        lax.all_gather(joined_w, ("section", "ctx"), axis=0, tiled=True),
        lax.all_gather(output_w, ("section", "ctx"), axis=0, tiled=True),
    )


def attend(inputs, joined_w, output_w, gain_rows, q_gain, k_gain):
    tok_rows = inputs.shape[0]
    groups = QH // KVH
    q_width = QH * HD
    k_width = KVH * HD
    score_scale = float(HD) ** (-0.5)
    widened = inputs.astype(jnp.float32)
    factor = lax.rsqrt(jnp.mean(widened * widened, axis=-1, keepdims=True) + 1e-06)
    normed = (widened * factor * gain_rows[0]).astype(jnp.bfloat16)
    projected = jnp.dot(normed, joined_w, preferred_element_type=jnp.float32)
    queries = qk_normal(projected[:, :q_width].reshape(tok_rows, KVH, groups, HD), q_gain)
    key_rows = qk_normal(
        projected[:, q_width : q_width + k_width].reshape(tok_rows, KVH, HD), k_gain
    )
    key_rows = key_rows.reshape(tok_rows, k_width)
    val_rows = projected[:, q_width + k_width :].astype(jnp.bfloat16)

    def add_block(running, key_block, val_block):
        scores = (
            jnp.einsum("tkgd,skd->tkgs", queries, key_block, preferred_element_type=jnp.float32)
            * score_scale
        )
        weights = jnp.exp(scores)
        numerator = running[0] + jnp.einsum(
            "tkgs,skd->tkgd",
            weights.astype(jnp.bfloat16),
            val_block,
            preferred_element_type=jnp.float32,
        )
        return (numerator, running[1] + jnp.sum(weights, axis=-1))

    initial = (
        jnp.zeros((tok_rows, KVH, groups, HD), jnp.float32),
        jnp.zeros((tok_rows, KVH, groups), jnp.float32),
    )
    running = initial
    pieces = (
        lax.all_gather(key_rows, "ctx", axis=0, tiled=True),
        lax.all_gather(val_rows, "ctx", axis=0, tiled=True),
    )
    row_count = pieces[0].shape[0]
    key_piece = pieces[0].reshape(row_count, KVH, HD)
    val_piece = pieces[1].reshape(row_count, KVH, HD)
    key_blocks = key_piece.reshape(row_count // 256, 256, KVH, HD)
    val_blocks = val_piece.reshape(row_count // 256, 256, KVH, HD)

    def step_block(state_pair, block_pair):
        return (add_block(state_pair, block_pair[0], block_pair[1]), None)

    running, unused = lax.scan(step_block, running, (key_blocks, val_blocks))
    numerator, denominator = running
    attended = (numerator / denominator[..., None]).astype(jnp.bfloat16).reshape(tok_rows, q_width)
    update = lax.dot_general(
        attended, output_w, (((1,), (1,)), ((), ())), preferred_element_type=jnp.float32
    )
    return (widened + gain_rows[1] * update).astype(jnp.bfloat16)


def per_device(
    latent_state, lead_step, tail_qkv, tail_out, head_qkv, head_out, modulation, qk_gain
):
    section_pos = lax.axis_index("section")
    section_count = lax.axis_size("section")
    lead_now = lax.dynamic_index_in_dim(lead_step, section_pos, 0, keepdims=False)
    sender = jnp.mod(section_pos - 1 + section_count, section_count)
    lead_next = lax.dynamic_index_in_dim(lead_step, sender, 0, keepdims=False) + 1
    tail_rows = lax.dynamic_index_in_dim(modulation[0], lead_now, 1, keepdims=False)
    head_rows = lax.dynamic_index_in_dim(modulation[1], lead_next, 1, keepdims=False)
    tail_weights = fetch_weights(tail_qkv, tail_out)
    tail_new = attend(
        latent_state[0], tail_weights[0], tail_weights[1], tail_rows, qk_gain[0, 0], qk_gain[0, 1]
    )
    arrived = passed_along(tail_new, "section", 1)
    head_weights = fetch_weights(head_qkv, head_out)
    head_new = attend(
        arrived, head_weights[0], head_weights[1], head_rows, qk_gain[1, 0], qk_gain[1, 1]
    )
    return (tail_new[None], head_new[None])


EPS = 1e-06
MESH = pl.DeviceIdType.MESH


def receive_slots(zs):
    names = []
    for piece in range(4):
        names += [(piece, side, d) for side in "xy" for d in range(zs)]
        names += [(piece, "xd"), (piece, "yd")]
        names += [(piece, "sib", j) for j in range(4)]
    for layer in range(2):
        names += [("kvs", layer, d) for d in range(zs)]
    names += [("state",)] + [("attended", h) for h in range(KVH)]
    return {name: i for i, name in enumerate(names)}


def rollout_kernel(
    zs, lead_ref, x_hbm, tq_ref, to_ref, hq_ref, ho_ref, mod_hbm, qkg_hbm,
    tail_ref, head_ref,
    wtq, wto, whq, who, kvb, qbuf, nbuf, abuf, afar, came, num, den, x_ref, mod_ref, qkg_ref,
    send_sems, recv_sems, z_sems, own_sems,
):
    slots = receive_slots(zs)
    sec = lax.axis_index("section")
    pos = lax.axis_index("ctx")
    z = pos // 2
    k = pos % 2
    sx = sec + 1 - 2 * (sec % 2)
    sy = (sec + 2) % 4
    sd = (sx + 2) % 4
    nxt = (sec + 1) % 4
    prev = (sec + 3) % 4
    half = zs // 2
    tok = x_ref.shape[1]
    shards = (tq_ref, to_ref, hq_ref, ho_ref)
    full = (wtq, wto, whq, who)
    sibling = (sec, 2 * z + 1 - k)
    x_peer = (sx, pos)
    y_peer = (sy, pos)
    z_up = (sec, 2 * ((z + 1) % zs) + k)
    z_down = (sec, 2 * ((z + zs - 1) % zs) + k)
    z_from = [z, z + 1 - 2 * (z % 2), 2 - z // 2, 3 - 3 * (z // 2)]

    sends = []

    def send(src, dst, name, device):
        copy = pltpu.make_async_remote_copy(
            src_ref=src, dst_ref=dst,
            send_sem=send_sems.at[len(sends)], recv_sem=recv_sems.at[slots[name]],
            device_id=device, device_id_type=MESH,
        )
        copy.start()
        sends.append((None, copy.wait_send))

    def send_z(src, dst, row, owner, up):
        slot = len(sends)
        goes = (owner <= z) & (z < zs - 1) if up else (owner >= z) & (z > 0)

        def copy():
            return pltpu.make_async_remote_copy(
                src_ref=src, dst_ref=dst,
                send_sem=send_sems.at[slot], recv_sem=z_sems.at[row, owner],
                device_id=z_up if up else z_down, device_id_type=MESH,
            )

        @pl.when(goes)
        def _():
            copy().start()

        sends.append((goes, lambda: copy().wait_send()))

    def receive_z(dst, row, owner):
        pltpu.make_async_remote_copy(
            src_ref=dst, dst_ref=dst,
            send_sem=send_sems.at[0], recv_sem=z_sems.at[row, owner],
            device_id=sibling, device_id_type=MESH,
        ).wait_recv()

    def receive(dst, name):
        pltpu.make_async_remote_copy(
            src_ref=dst, dst_ref=dst,
            send_sem=send_sems.at[0], recv_sem=recv_sems.at[slots[name]],
            device_id=sibling, device_id_type=MESH,
        ).wait_recv()

    own_copies = [
        pltpu.make_async_copy(shards[p], full[p].at[sec, z, k], own_sems.at[p]) for p in range(4)
    ]

    def send_own(p):
        w = full[p]
        for up in (True, False):
            send_z(shards[p], w.at[sec, z, k], p, z, up)
        send(shards[p], w.at[sec, z, k], (p, "x", 0), x_peer)
        send(shards[p], w.at[sec, z, k], (p, "y", 0), y_peer)

    def forward_z(p):
        w = full[p]
        for d in range(1, zs):
            block = w.at[sec, z_from[d], k]
            receive_z(block, p, z_from[d])
            for up in (True, False):
                send_z(block, block, p, z_from[d], up)
            send(block, block, (p, "x", d), x_peer)
            send(block, block, (p, "y", d), y_peer)
        own_copies[p].wait()
        column = w.at[sec, :, k]
        send(column, column, (p, "sib", 0), sibling)

    def forward_xy(p):
        w = full[p]
        for d in range(zs):
            receive(w.at[sx, z_from[d], k], (p, "x", d))
        part = w.at[sx, pl.ds(0, half), k]
        send(part, part, (p, "yd"), y_peer)
        column = w.at[sx, :, k]
        send(column, column, (p, "sib", 1), sibling)
        for d in range(zs):
            receive(w.at[sy, z_from[d], k], (p, "y", d))
        part = w.at[sy, pl.ds(half, zs - half), k]
        send(part, part, (p, "xd"), x_peer)
        column = w.at[sy, :, k]
        send(column, column, (p, "sib", 2), sibling)

    def finish(p):
        w = full[p]
        receive(w.at[sd, pl.ds(0, half), k], (p, "yd"))
        receive(w.at[sd, pl.ds(half, zs - half), k], (p, "xd"))
        column = w.at[sd, :, k]
        send(column, column, (p, "sib", 3), sibling)
        for j, owner in enumerate((sec, sx, sy, sd)):
            receive(w.at[owner, :, 1 - k], (p, "sib", j))

    barrier = pltpu.get_barrier_semaphore()
    partners = [z_up, z_down, sibling, x_peer, y_peer, (sd, pos)]
    for device in partners:
        pl.semaphore_signal(barrier, inc=1, device_id=device, device_id_type=MESH)
    small_copies = [
        pltpu.make_async_copy(src, dst, own_sems.at[4 + i])
        for i, (src, dst) in enumerate(((x_hbm, x_ref), (mod_hbm, mod_ref), (qkg_hbm, qkg_ref)))
    ]
    for copy in small_copies + own_copies:
        copy.start()
    pl.semaphore_wait(barrier, len(partners))

    def normalize(rows, gain):
        wide = rows.astype(jnp.float32)
        factor = lax.rsqrt(jnp.mean(wide * wide, axis=-1, keepdims=True) + EPS)
        nbuf[...] = (wide * factor * gain).astype(jnp.bfloat16)

    def project(w, first):
        weights = w[:, :, :, :, first : first + 256].reshape(-1, 256)
        return jnp.dot(nbuf[...], weights, preferred_element_type=jnp.float32)

    def head_normal(values, gain):
        factor = lax.rsqrt(jnp.mean(values * values, axis=-1, keepdims=True) + EPS)
        return (values * factor * gain).astype(jnp.bfloat16)

    def keys_values(w, layer):
        k_gain = qkg_ref[layer, pl.ds(1, 1), :]
        keys = project(w, QH * HD)
        block = kvb.at[layer, z, k]
        for h in range(KVH):
            block[:, h * HD : (h + 1) * HD] = head_normal(keys[:, h * HD : (h + 1) * HD], k_gain)
        block[:, KVH * HD :] = project(w, (QH + KVH) * HD).astype(jnp.bfloat16)
        for up in (True, False):
            send_z(block, block, 4 + layer, z, up)
        send(block, block, ("kvs", layer, 0), sibling)

    def queries(w, layer):
        q_gain = qkg_ref[layer, pl.ds(0, 1), :]
        for pair in range(QH // 2):
            both = project(w, pair * 2 * HD)
            for i in range(2):
                h = 2 * pair + i
                row = (h % 3) * tok
                qbuf[h // 3, row : row + tok, :] = head_normal(
                    both[:, i * HD : (i + 1) * HD], q_gain
                )

    def pass_keys(layer, d):
        block = kvb.at[layer, z_from[d], k]
        receive_z(block, 4 + layer, z_from[d])
        for up in (True, False):
            send_z(block, block, 4 + layer, z_from[d], up)
        send(block, block, ("kvs", layer, d), sibling)

    def attend_block(layer, d):
        receive(kvb.at[layer, z_from[d], 1 - k], ("kvs", layer, d))
        both = kvb[layer, z_from[d]].reshape(2 * tok, 2 * KVH * HD)
        for h in range(KVH):
            scores = lax.dot_general(
                qbuf[h], both[:, h * HD : (h + 1) * HD], (((1,), (1,)), ((), ())),
                preferred_element_type=jnp.float32,
            )
            weights = jnp.exp(scores * float(HD) ** (-0.5))
            total = jnp.sum(weights, axis=-1, keepdims=True)
            mixed = jnp.dot(
                weights.astype(jnp.bfloat16),
                both[:, (KVH + h) * HD : (KVH + h + 1) * HD],
                preferred_element_type=jnp.float32,
            )
            if d > 0:
                mixed = mixed + num[h]
                total = total + den[h]
            if d < zs - 1:
                num[h] = mixed
                den[h] = total
            else:
                result = (mixed / total).astype(jnp.bfloat16)
                for i in range(3):
                    abuf[layer, h, :, i * HD : (i + 1) * HD] = result[i * tok : (i + 1) * tok]
                if layer == 1:
                    send(abuf.at[1, h], afar.at[h], ("attended", h), (nxt, pos))

    def finish_layer(w, attended_ref, rows_ref, gate, out_ref):
        for j in range(4):
            weights = w[j].reshape(-1, QH * HD)
            width = weights.shape[0]
            columns = slice(j * width, (j + 1) * width)
            part = weights.shape[1] // KVH
            update = sum(
                lax.dot_general(
                    attended_ref[h], weights[:, h * part : (h + 1) * part],
                    (((1,), (1,)), ((), ())), preferred_element_type=jnp.float32,
                )
                for h in range(KVH)
            )
            wide = rows_ref[:, columns].astype(jnp.float32)
            out_ref[:, columns] = (wide + gate[:, columns] * update).astype(jnp.bfloat16)

    lead_now = lead_ref[sec]
    lead_came = lead_ref[prev]

    send_own(0)
    for copy in small_copies:
        copy.wait()
    normalize(x_ref[0], mod_ref[0, lead_now, pl.ds(0, 1), :])
    forward_z(0)
    send_own(1)
    forward_xy(0)
    forward_z(1)
    send_own(2)
    finish(0)
    keys_values(wtq, 0)
    forward_z(2)
    queries(wtq, 0)
    pass_keys(0, 1)
    forward_xy(1)
    pass_keys(0, 2)
    send_own(3)
    attend_block(0, 0)
    attend_block(0, 1)
    pass_keys(0, 3)
    attend_block(0, 2)
    attend_block(0, 3)
    forward_xy(2)
    forward_z(3)
    finish(1)
    finish_layer(wto, abuf.at[0], x_ref.at[0], mod_ref[0, lead_now, pl.ds(1, 1), :], tail_ref.at[0])
    send(tail_ref.at[0], came, ("state",), (nxt, pos))
    normalize(tail_ref[0], mod_ref[1, lead_now + 1, pl.ds(0, 1), :])
    finish(2)
    keys_values(whq, 1)
    queries(whq, 1)
    pass_keys(1, 1)
    attend_block(1, 0)
    pass_keys(1, 2)
    attend_block(1, 1)
    forward_xy(3)
    pass_keys(1, 3)
    attend_block(1, 2)
    attend_block(1, 3)
    finish(3)
    receive(came, ("state",))
    for h in range(KVH):
        receive(afar.at[h], ("attended", h))
    finish_layer(who, afar, came, mod_ref[1, lead_came + 1, pl.ds(1, 1), :], head_ref.at[0])
    for goes, wait in sends:
        if goes is None:
            wait()
        else:
            pl.when(goes)(wait)


def fused(latent_state, lead_step, tail_qkv, tail_out, head_qkv, head_out, modulation, qk_gain):
    ctx = lax.axis_size("ctx")
    zs = ctx // 2
    rows = tail_qkv.shape[0]
    tok = latent_state.shape[1]
    wide = latent_state.shape[2]
    joined = tail_qkv.shape[1]
    inner = tail_out.shape[1]
    n_slots = len(receive_slots(zs))
    by_lead = jnp.swapaxes(modulation, 1, 2)
    vmem = pl.BlockSpec(memory_space=pltpu.VMEM)
    smem = pl.BlockSpec(memory_space=pltpu.SMEM)
    state = jax.ShapeDtypeStruct(latent_state.shape, jnp.bfloat16)
    return pl.pallas_call(
        functools.partial(rollout_kernel, zs),
        out_shape=(state, state),
        in_specs=[smem] + [pl.BlockSpec(memory_space=pltpu.HBM)] * 7,
        out_specs=(vmem, vmem),
        scratch_shapes=[
            pltpu.VMEM((4, zs, 2, rows, joined), jnp.bfloat16),
            pltpu.VMEM((4, zs, 2, rows, inner), jnp.bfloat16),
            pltpu.VMEM((4, zs, 2, rows, joined), jnp.bfloat16),
            pltpu.VMEM((4, zs, 2, rows, inner), jnp.bfloat16),
            pltpu.VMEM((2, zs, 2, tok, 2 * KVH * HD), jnp.bfloat16),
            pltpu.VMEM((KVH, QH // KVH * tok, HD), jnp.bfloat16),
            pltpu.VMEM((tok, wide), jnp.bfloat16),
            pltpu.VMEM((2, KVH, tok, QH // KVH * HD), jnp.bfloat16),
            pltpu.VMEM((KVH, tok, QH // KVH * HD), jnp.bfloat16),
            pltpu.VMEM((tok, wide), jnp.bfloat16),
            pltpu.VMEM((KVH, QH // KVH * tok, HD), jnp.float32),
            pltpu.VMEM((KVH, QH // KVH * tok, 1), jnp.float32),
            pltpu.VMEM(latent_state.shape, jnp.bfloat16),
            pltpu.VMEM(by_lead.shape, jnp.float32),
            pltpu.VMEM(qk_gain.shape, jnp.float32),
            pltpu.SemaphoreType.DMA((n_slots + 6 * 2 * zs,)),
            pltpu.SemaphoreType.DMA((n_slots,)),
            pltpu.SemaphoreType.DMA((6, zs)),
            pltpu.SemaphoreType.DMA((7,)),
        ],
        compiler_params=pltpu.CompilerParams(
            collective_id=0, has_side_effects=True, vmem_limit_bytes=60 * 1024 * 1024
        ),
    )(lead_step, latent_state, tail_qkv, tail_out, head_qkv, head_out, by_lead, qk_gain)


def solution(mesh):
    in_specs = (
        P("section", "ctx", None),
        P(),
        P(("section", "ctx"), None),
        P(("section", "ctx"), None),
        P(("section", "ctx"), None),
        P(("section", "ctx"), None),
        P(),
        P(),
    )
    out_specs = (P("section", "ctx", None), P("section", "ctx", None))
    planar = mesh.shape["section"] == 4 and mesh.shape["ctx"] == 8
    return jax.shard_map(
        fused if planar else per_device, mesh=mesh, in_specs=in_specs, out_specs=out_specs, check_vma=False
    )
```

```python
import functools

import jax
import jax.numpy as jnp
from jax import lax
from jax.experimental import pallas as pl
from jax.experimental.pallas import tpu as pltpu
from jax.sharding import PartitionSpec as P

QH = 6
KVH = 2
HD = 128


def passed_along(x, axis, by):
    peers = lax.axis_size(axis)
    return lax.ppermute(x, axis, [(i, (i + by) % peers) for i in range(peers)])


def qk_normal(values, gain_row):
    factor = lax.rsqrt(jnp.mean(values * values, axis=-1, keepdims=True) + 1e-06)
    return (values * factor * gain_row).astype(jnp.bfloat16)


def fetch_weights(joined_w, output_w):
    return (
        lax.all_gather(joined_w, ("section", "ctx"), axis=0, tiled=True),
        lax.all_gather(output_w, ("section", "ctx"), axis=0, tiled=True),
    )


def attend(inputs, joined_w, output_w, gain_rows, q_gain, k_gain):
    tok_rows = inputs.shape[0]
    groups = QH // KVH
    q_width = QH * HD
    k_width = KVH * HD
    score_scale = float(HD) ** (-0.5)
    widened = inputs.astype(jnp.float32)
    factor = lax.rsqrt(jnp.mean(widened * widened, axis=-1, keepdims=True) + 1e-06)
    normed = (widened * factor * gain_rows[0]).astype(jnp.bfloat16)
    projected = jnp.dot(normed, joined_w, preferred_element_type=jnp.float32)
    queries = qk_normal(projected[:, :q_width].reshape(tok_rows, KVH, groups, HD), q_gain)
    key_rows = qk_normal(
        projected[:, q_width : q_width + k_width].reshape(tok_rows, KVH, HD), k_gain
    )
    key_rows = key_rows.reshape(tok_rows, k_width)
    val_rows = projected[:, q_width + k_width :].astype(jnp.bfloat16)

    def add_block(running, key_block, val_block):
        scores = (
            jnp.einsum("tkgd,skd->tkgs", queries, key_block, preferred_element_type=jnp.float32)
            * score_scale
        )
        weights = jnp.exp(scores)
        numerator = running[0] + jnp.einsum(
            "tkgs,skd->tkgd",
            weights.astype(jnp.bfloat16),
            val_block,
            preferred_element_type=jnp.float32,
        )
        return (numerator, running[1] + jnp.sum(weights, axis=-1))

    initial = (
        jnp.zeros((tok_rows, KVH, groups, HD), jnp.float32),
        jnp.zeros((tok_rows, KVH, groups), jnp.float32),
    )
    running = initial
    pieces = (
        lax.all_gather(key_rows, "ctx", axis=0, tiled=True),
        lax.all_gather(val_rows, "ctx", axis=0, tiled=True),
    )
    row_count = pieces[0].shape[0]
    key_piece = pieces[0].reshape(row_count, KVH, HD)
    val_piece = pieces[1].reshape(row_count, KVH, HD)
    key_blocks = key_piece.reshape(row_count // 256, 256, KVH, HD)
    val_blocks = val_piece.reshape(row_count // 256, 256, KVH, HD)

    def step_block(state_pair, block_pair):
        return (add_block(state_pair, block_pair[0], block_pair[1]), None)

    running, unused = lax.scan(step_block, running, (key_blocks, val_blocks))
    numerator, denominator = running
    attended = (numerator / denominator[..., None]).astype(jnp.bfloat16).reshape(tok_rows, q_width)
    update = lax.dot_general(
        attended, output_w, (((1,), (1,)), ((), ())), preferred_element_type=jnp.float32
    )
    return (widened + gain_rows[1] * update).astype(jnp.bfloat16)


def per_device(
    latent_state, lead_step, tail_qkv, tail_out, head_qkv, head_out, modulation, qk_gain
):
    section_pos = lax.axis_index("section")
    section_count = lax.axis_size("section")
    lead_now = lax.dynamic_index_in_dim(lead_step, section_pos, 0, keepdims=False)
    sender = jnp.mod(section_pos - 1 + section_count, section_count)
    lead_next = lax.dynamic_index_in_dim(lead_step, sender, 0, keepdims=False) + 1
    tail_rows = lax.dynamic_index_in_dim(modulation[0], lead_now, 1, keepdims=False)
    head_rows = lax.dynamic_index_in_dim(modulation[1], lead_next, 1, keepdims=False)
    tail_weights = fetch_weights(tail_qkv, tail_out)
    tail_new = attend(
        latent_state[0], tail_weights[0], tail_weights[1], tail_rows, qk_gain[0, 0], qk_gain[0, 1]
    )
    arrived = passed_along(tail_new, "section", 1)
    head_weights = fetch_weights(head_qkv, head_out)
    head_new = attend(
        arrived, head_weights[0], head_weights[1], head_rows, qk_gain[1, 0], qk_gain[1, 1]
    )
    return (tail_new[None], head_new[None])


EPS = 1e-06
MESH = pl.DeviceIdType.MESH


def receive_slots(zs):
    names = []
    for piece in range(4):
        names += [(piece, side, d) for side in "xy" for d in range(zs)]
        names += [(piece, "xd"), (piece, "yd")]
        names += [(piece, "sib", j) for j in range(4)]
    names += [(3, "corner")]
    for layer in range(2):
        names += [("kvs", layer, d) for d in range(zs)]
    names += [("state",)] + [("attended", h) for h in range(KVH)]
    return {name: i for i, name in enumerate(names)}


def rollout_kernel(
    zs, lead_ref, x_hbm, tq_ref, to_ref, hq_ref, ho_ref, mod_hbm, qkg_hbm,
    tail_ref, head_ref,
    wtq, wto, whq, who, kvb, qbuf, nbuf, abuf, afar, came, num, den, x_ref, mod_ref, qkg_ref,
    send_sems, recv_sems, z_sems, own_sems,
):
    slots = receive_slots(zs)
    sec = lax.axis_index("section")
    pos = lax.axis_index("ctx")
    z = pos // 2
    k = pos % 2
    sx = sec + 1 - 2 * (sec % 2)
    sy = (sec + 2) % 4
    sd = (sx + 2) % 4
    nxt = (sec + 1) % 4
    prev = (sec + 3) % 4
    half = zs // 2
    tok = x_ref.shape[1]
    shards = (tq_ref, to_ref, hq_ref, ho_ref)
    full = (wtq, wto, whq, who)
    sibling = (sec, 2 * z + 1 - k)
    x_peer = (sx, pos)
    y_peer = (sy, pos)
    z_up = (sec, 2 * ((z + 1) % zs) + k)
    z_down = (sec, 2 * ((z + zs - 1) % zs) + k)
    z_from = [z, z + 1 - 2 * (z % 2), 2 - z // 2, 3 - 3 * (z // 2)]

    sends = []

    def send(src, dst, name, device):
        copy = pltpu.make_async_remote_copy(
            src_ref=src, dst_ref=dst,
            send_sem=send_sems.at[len(sends)], recv_sem=recv_sems.at[slots[name]],
            device_id=device, device_id_type=MESH,
        )
        copy.start()
        sends.append((None, copy.wait_send))

    def send_z(src, dst, row, owner, up):
        slot = len(sends)
        goes = (owner <= z) & (z < zs - 1) if up else (owner >= z) & (z > 0)

        def copy():
            return pltpu.make_async_remote_copy(
                src_ref=src, dst_ref=dst,
                send_sem=send_sems.at[slot], recv_sem=z_sems.at[row, owner],
                device_id=z_up if up else z_down, device_id_type=MESH,
            )

        @pl.when(goes)
        def _():
            copy().start()

        sends.append((goes, lambda: copy().wait_send()))

    def receive_z(dst, row, owner):
        pltpu.make_async_remote_copy(
            src_ref=dst, dst_ref=dst,
            send_sem=send_sems.at[0], recv_sem=z_sems.at[row, owner],
            device_id=sibling, device_id_type=MESH,
        ).wait_recv()

    def receive(dst, name):
        pltpu.make_async_remote_copy(
            src_ref=dst, dst_ref=dst,
            send_sem=send_sems.at[0], recv_sem=recv_sems.at[slots[name]],
            device_id=sibling, device_id_type=MESH,
        ).wait_recv()

    own_copies = [
        pltpu.make_async_copy(shards[p], full[p].at[sec, z, k], own_sems.at[p]) for p in range(4)
    ]

    def send_own(p):
        w = full[p]
        for up in (True, False):
            send_z(shards[p], w.at[sec, z, k], p, z, up)
        send(shards[p], w.at[sec, z, k], (p, "x", 0), x_peer)
        send(shards[p], w.at[sec, z, k], (p, "y", 0), y_peer)

    def forward_z(p):
        w = full[p]
        for d in range(1, zs):
            block = w.at[sec, z_from[d], k]
            receive_z(block, p, z_from[d])
            for up in (True, False):
                send_z(block, block, p, z_from[d], up)
            send(block, block, (p, "x", d), x_peer)
            send(block, block, (p, "y", d), y_peer)
        own_copies[p].wait()
        column = w.at[sec, :, k]
        send(column, column, (p, "sib", 0), sibling)

    def forward_xy(p):
        w = full[p]
        for d in range(zs):
            receive(w.at[sx, z_from[d], k], (p, "x", d))
        part = w.at[sx, pl.ds(0, half), k]
        send(part, part, (p, "yd"), y_peer)
        column = w.at[sx, :, k]
        send(column, column, (p, "sib", 1), sibling)
        for d in range(zs):
            receive(w.at[sy, z_from[d], k], (p, "y", d))
        part = w.at[sy, pl.ds(half, zs - half), k]
        send(part, part, (p, "xd"), x_peer)
        column = w.at[sy, :, k]
        send(column, column, (p, "sib", 2), sibling)

    def finish(p):
        w = full[p]
        receive(w.at[sd, pl.ds(0, half), k], (p, "yd"))
        receive(w.at[sd, pl.ds(half, zs - half), k], (p, "xd"))
        column = w.at[sd, :, k]
        send(column, column, (p, "sib", 3), sibling)
        for j, owner in enumerate((sec, sx, sy, sd)):
            receive(w.at[owner, :, 1 - k], (p, "sib", j))

    def start_plane(p):
        own_copies[p].wait()
        block = full[p].at[sec, z, k]
        send(block, block, (p, "x", 0), x_peer)
        send(block, block, (p, "y", 0), y_peer)

    def close_plane(p):
        w = full[p]
        receive(w.at[sx, z, k], (p, "x", 0))
        receive(w.at[sy, z, k], (p, "y", 0))
        block = w.at[sx + k * (sy - sx), z, k]
        send(block, block, (p, "corner"), (sy + k * (sx - sy), pos))

    def forward_line(p, d):
        plane = full[p].at[:, z_from[d], k]
        if d == 0:
            receive(full[p].at[sd, z, k], (p, "corner"))
        else:
            receive_z(plane, p, z_from[d])
        for up in (True, False):
            send_z(plane, plane, p, z_from[d], up)
        send(plane, plane, (p, "sib", d), sibling)

    def finish_line(p):
        for d in range(zs):
            receive(full[p].at[:, z_from[d], 1 - k], (p, "sib", d))

    barrier = pltpu.get_barrier_semaphore()
    partners = [z_up, z_down, sibling, x_peer, y_peer, (sd, pos)]
    for device in partners:
        pl.semaphore_signal(barrier, inc=1, device_id=device, device_id_type=MESH)
    small_copies = [
        pltpu.make_async_copy(src, dst, own_sems.at[4 + i])
        for i, (src, dst) in enumerate(((x_hbm, x_ref), (mod_hbm, mod_ref), (qkg_hbm, qkg_ref)))
    ]
    for copy in small_copies + own_copies:
        copy.start()
    pl.semaphore_wait(barrier, len(partners))

    def normalize(rows, gain):
        wide = rows.astype(jnp.float32)
        factor = lax.rsqrt(jnp.mean(wide * wide, axis=-1, keepdims=True) + EPS)
        nbuf[...] = (wide * factor * gain).astype(jnp.bfloat16)

    def project(w, first):
        weights = w[:, :, :, :, first : first + 256].reshape(-1, 256)
        return jnp.dot(nbuf[...], weights, preferred_element_type=jnp.float32)

    def head_normal(values, gain):
        factor = lax.rsqrt(jnp.mean(values * values, axis=-1, keepdims=True) + EPS)
        return (values * factor * gain).astype(jnp.bfloat16)

    def keys_values(w, layer):
        k_gain = qkg_ref[layer, pl.ds(1, 1), :]
        keys = project(w, QH * HD)
        block = kvb.at[layer, z, k]
        for h in range(KVH):
            block[:, h * HD : (h + 1) * HD] = head_normal(keys[:, h * HD : (h + 1) * HD], k_gain)
        block[:, KVH * HD :] = project(w, (QH + KVH) * HD).astype(jnp.bfloat16)
        for up in (True, False):
            send_z(block, block, 4 + layer, z, up)
        send(block, block, ("kvs", layer, 0), sibling)

    def queries(w, layer):
        q_gain = qkg_ref[layer, pl.ds(0, 1), :]
        for pair in range(QH // 2):
            both = project(w, pair * 2 * HD)
            for i in range(2):
                h = 2 * pair + i
                row = (h % 3) * tok
                qbuf[h // 3, row : row + tok, :] = head_normal(
                    both[:, i * HD : (i + 1) * HD], q_gain
                )

    def pass_keys(layer, d):
        block = kvb.at[layer, z_from[d], k]
        receive_z(block, 4 + layer, z_from[d])
        for up in (True, False):
            send_z(block, block, 4 + layer, z_from[d], up)
        send(block, block, ("kvs", layer, d), sibling)

    def attend_block(layer, d):
        receive(kvb.at[layer, z_from[d], 1 - k], ("kvs", layer, d))
        both = kvb[layer, z_from[d]].reshape(2 * tok, 2 * KVH * HD)
        for h in range(KVH):
            scores = lax.dot_general(
                qbuf[h], both[:, h * HD : (h + 1) * HD], (((1,), (1,)), ((), ())),
                preferred_element_type=jnp.float32,
            )
            weights = jnp.exp(scores * float(HD) ** (-0.5))
            total = jnp.sum(weights, axis=-1, keepdims=True)
            mixed = jnp.dot(
                weights.astype(jnp.bfloat16),
                both[:, (KVH + h) * HD : (KVH + h + 1) * HD],
                preferred_element_type=jnp.float32,
            )
            if d > 0:
                mixed = mixed + num[h]
                total = total + den[h]
            if d < zs - 1:
                num[h] = mixed
                den[h] = total
            else:
                result = (mixed / total).astype(jnp.bfloat16)
                for i in range(3):
                    abuf[layer, h, :, i * HD : (i + 1) * HD] = result[i * tok : (i + 1) * tok]
                if layer == 1:
                    send(abuf.at[1, h], afar.at[h], ("attended", h), (nxt, pos))

    def finish_layer(w, attended_ref, rows_ref, gate, out_ref):
        for j in range(4):
            weights = w[j].reshape(-1, QH * HD)
            width = weights.shape[0]
            columns = slice(j * width, (j + 1) * width)
            part = weights.shape[1] // KVH
            update = sum(
                lax.dot_general(
                    attended_ref[h], weights[:, h * part : (h + 1) * part],
                    (((1,), (1,)), ((), ())), preferred_element_type=jnp.float32,
                )
                for h in range(KVH)
            )
            wide = rows_ref[:, columns].astype(jnp.float32)
            out_ref[:, columns] = (wide + gate[:, columns] * update).astype(jnp.bfloat16)

    lead_now = lead_ref[sec]
    lead_came = lead_ref[prev]

    send_own(0)
    for copy in small_copies:
        copy.wait()
    normalize(x_ref[0], mod_ref[0, lead_now, pl.ds(0, 1), :])
    forward_z(0)
    send_own(1)
    forward_xy(0)
    forward_z(1)
    send_own(2)
    start_plane(3)
    finish(0)
    keys_values(wtq, 0)
    forward_z(2)
    queries(wtq, 0)
    pass_keys(0, 1)
    close_plane(3)
    forward_xy(1)
    pass_keys(0, 2)
    attend_block(0, 0)
    attend_block(0, 1)
    pass_keys(0, 3)
    forward_line(3, 0)
    attend_block(0, 2)
    attend_block(0, 3)
    forward_xy(2)
    finish(1)
    forward_line(3, 1)
    finish_layer(wto, abuf.at[0], x_ref.at[0], mod_ref[0, lead_now, pl.ds(1, 1), :], tail_ref.at[0])
    send(tail_ref.at[0], came, ("state",), (nxt, pos))
    normalize(tail_ref[0], mod_ref[1, lead_now + 1, pl.ds(0, 1), :])
    forward_line(3, 2)
    finish(2)
    keys_values(whq, 1)
    queries(whq, 1)
    forward_line(3, 3)
    pass_keys(1, 1)
    attend_block(1, 0)
    pass_keys(1, 2)
    attend_block(1, 1)
    pass_keys(1, 3)
    attend_block(1, 2)
    attend_block(1, 3)
    finish_line(3)
    receive(came, ("state",))
    for h in range(KVH):
        receive(afar.at[h], ("attended", h))
    finish_layer(who, afar, came, mod_ref[1, lead_came + 1, pl.ds(1, 1), :], head_ref.at[0])
    for goes, wait in sends:
        if goes is None:
            wait()
        else:
            pl.when(goes)(wait)


def fused(latent_state, lead_step, tail_qkv, tail_out, head_qkv, head_out, modulation, qk_gain):
    ctx = lax.axis_size("ctx")
    zs = ctx // 2
    rows = tail_qkv.shape[0]
    tok = latent_state.shape[1]
    wide = latent_state.shape[2]
    joined = tail_qkv.shape[1]
    inner = tail_out.shape[1]
    n_slots = len(receive_slots(zs))
    by_lead = jnp.swapaxes(modulation, 1, 2)
    vmem = pl.BlockSpec(memory_space=pltpu.VMEM)
    smem = pl.BlockSpec(memory_space=pltpu.SMEM)
    state = jax.ShapeDtypeStruct(latent_state.shape, jnp.bfloat16)
    return pl.pallas_call(
        functools.partial(rollout_kernel, zs),
        out_shape=(state, state),
        in_specs=[smem] + [pl.BlockSpec(memory_space=pltpu.HBM)] * 7,
        out_specs=(vmem, vmem),
        scratch_shapes=[
            pltpu.VMEM((4, zs, 2, rows, joined), jnp.bfloat16),
            pltpu.VMEM((4, zs, 2, rows, inner), jnp.bfloat16),
            pltpu.VMEM((4, zs, 2, rows, joined), jnp.bfloat16),
            pltpu.VMEM((4, zs, 2, rows, inner), jnp.bfloat16),
            pltpu.VMEM((2, zs, 2, tok, 2 * KVH * HD), jnp.bfloat16),
            pltpu.VMEM((KVH, QH // KVH * tok, HD), jnp.bfloat16),
            pltpu.VMEM((tok, wide), jnp.bfloat16),
            pltpu.VMEM((2, KVH, tok, QH // KVH * HD), jnp.bfloat16),
            pltpu.VMEM((KVH, tok, QH // KVH * HD), jnp.bfloat16),
            pltpu.VMEM((tok, wide), jnp.bfloat16),
            pltpu.VMEM((KVH, QH // KVH * tok, HD), jnp.float32),
            pltpu.VMEM((KVH, QH // KVH * tok, 1), jnp.float32),
            pltpu.VMEM(latent_state.shape, jnp.bfloat16),
            pltpu.VMEM(by_lead.shape, jnp.float32),
            pltpu.VMEM(qk_gain.shape, jnp.float32),
            pltpu.SemaphoreType.DMA((n_slots + 6 * 2 * zs,)),
            pltpu.SemaphoreType.DMA((n_slots,)),
            pltpu.SemaphoreType.DMA((6, zs)),
            pltpu.SemaphoreType.DMA((7,)),
        ],
        compiler_params=pltpu.CompilerParams(
            collective_id=0, has_side_effects=True, vmem_limit_bytes=60 * 1024 * 1024
        ),
    )(lead_step, latent_state, tail_qkv, tail_out, head_qkv, head_out, by_lead, qk_gain)


def solution(mesh):
    in_specs = (
        P("section", "ctx", None),
        P(),
        P(("section", "ctx"), None),
        P(("section", "ctx"), None),
        P(("section", "ctx"), None),
        P(("section", "ctx"), None),
        P(),
        P(),
    )
    out_specs = (P("section", "ctx", None), P("section", "ctx", None))
    planar = mesh.shape["section"] == 4 and mesh.shape["ctx"] == 8
    return jax.shard_map(
        fused if planar else per_device, mesh=mesh, in_specs=in_specs, out_specs=out_specs, check_vma=False
    )
```
